128 devices in a mesh: shard: 128 (over x, y, z, core).
Axes of the slice: x: 4, y: 4, z: 4, core: 2. Of those that a mesh axis runs over, the one named last changes fastest.
Arguments:
- features: bfloat16 [131072, 128], P('shard'), may hold values from -6 to 6
- conv_weight: bfloat16 [27, 128, 128], replicated, may hold values from -0.125 to 0.125
- down_weight: bfloat16 [8, 128, 256], replicated, may hold values from -0.25 to 0.25
- neighbour_map: int32 [27, 131072], P(None, 'shard'), may hold values from 0 to 1280, as said below
- halo_rows: int32 [4, 8192], P(None, 'shard'), may hold values from 0 to 1024, as said below
- child_map: int32 [8, 32768], P(None, 'shard'), may hold values from 0 to 1152, as said below
- child_rows: int32 [4, 4096], P(None, 'shard'), may hold values from 0 to 1024, as said below
- out_grad: bfloat16 [32768, 256], P('shard'), may hold values from -6 to 6
Outputs:
- coarse: bfloat16 [32768, 256], P('shard')
- input_grad: float32 [131072, 128], P('shard')
- conv_grad: float32 [27, 128, 128], replicated
- down_grad: float32 [8, 128, 256], replicated
The draws below stay inside these ranges and needn't reach their ends.
Inputs may be any that keep to these rules, and one draw needn't show every extreme that they name: `neighbour_map`: indices into the device's extended fine table: below 1024 a local voxel, 1024 + s*64 + c row c received in slot s, the largest value a missing neighbour. Offset 13 maps every voxel to itself. Rows received in slot s that a map reads are live entries of the sender's list. `halo_rows`: live entries come first in a slot, the rest are 1024; every slot toward a missing device is empty; the slot of offset +1 is full on every device that has a next device. `child_map`: as neighbour_map, for the extended hidden table with 32 rows per slot. `child_rows`: as halo_rows, with 32 rows per slot.
All inputs are finite; a program needn't handle non-finite values.
Results may differ from the reference program's by a relative error of at most 0.006.
Values may be sent and summed in bfloat16 or wider, within the bound.
A program may use at most 64 MiB of HBM per device.

```python
import math
import jax
import jax.numpy as jnp
from jax import lax

C1 = 128
C2 = 256
V_DEV = 1024
REACH = 2
P_DEV = 256
SLOTS = 4
CAP = 64
CAP2 = 32
VOXELS = 131072
PARENTS = 32768
N_SHARD = 128


def slot_offsets():
    return jnp.concatenate([jnp.arange(-REACH, 0, dtype=jnp.int32), jnp.arange(1, REACH + 1, dtype=jnp.int32)])


def slot_counts(key, capacity):
    counts = jax.random.randint(key, (N_SHARD, SLOTS), capacity // 2, capacity + 1)
    counts = counts.at[:, REACH].set(capacity)
    target = jnp.arange(N_SHARD, dtype=jnp.int32)[:, None] + slot_offsets()[None, :]
    return jnp.where((target >= 0) & (target < N_SHARD), counts, 0)


def send_lists(key, capacity):
    counts = slot_counts(key, capacity)
    picked = jax.random.randint(jax.random.fold_in(key, 7), (N_SHARD, SLOTS, capacity), 0, V_DEV)
    places = jnp.arange(capacity, dtype=jnp.int32)[None, None, :]
    sent_rows = jnp.where(places < counts[:, :, None], picked, V_DEV)
    return sent_rows.transpose(1, 0, 2).reshape(SLOTS, N_SHARD * capacity)


def index_map(key, counts, capacity, kernel_count, row_count):
    subkeys = jax.random.split(key, 4)
    shape_all = (N_SHARD, kernel_count, row_count)
    category = jax.random.randint(subkeys[0], shape_all, 0, 4)
    local_row = jax.random.randint(subkeys[1], shape_all, 0, V_DEV)
    slot_pick = jax.random.randint(subkeys[2], shape_all, 0, SLOTS)
    source = jnp.arange(N_SHARD, dtype=jnp.int32)[:, None, None] - slot_offsets()[slot_pick]
    in_range = (source >= 0) & (source < N_SHARD)
    available = jnp.where(in_range, counts[jnp.clip(source, 0, N_SHARD - 1), slot_pick], 0)
    position = jax.random.randint(subkeys[3], shape_all, 0, jnp.maximum(available, 1))
    absent = V_DEV + SLOTS * capacity
    halo_index = jnp.where(available > 0, V_DEV + slot_pick * capacity + position, absent)
    return jnp.where(category < 2, local_row, jnp.where(category == 2, halo_index, absent))


def draw_halo_rows(key, part):
    common = jax.random.fold_in(key, 11)
    return send_lists(common, CAP)


def draw_neighbour_map(key, part):
    common = jax.random.fold_in(key, 11)
    counts = slot_counts(common, CAP)
    own_key = jax.random.fold_in(key, 21)
    chosen = index_map(own_key, counts, CAP, 27, V_DEV)
    chosen = chosen.at[:, 13, :].set(jnp.arange(V_DEV, dtype=jnp.int32)[None, :])
    return chosen.transpose(1, 0, 2).reshape(27, N_SHARD * V_DEV)


def draw_child_rows(key, part):
    common = jax.random.fold_in(key, 31)
    return send_lists(common, CAP2)


def draw_child_map(key, part):
    common = jax.random.fold_in(key, 31)
    counts = slot_counts(common, CAP2)
    own_key = jax.random.fold_in(key, 41)
    chosen = index_map(own_key, counts, CAP2, 8, P_DEV)
    return chosen.transpose(1, 0, 2).reshape(8, N_SHARD * P_DEV)


def level_of(key, shape, cuts, low, high):
    gain = 1.0
    for axis_at, shards_of in cuts:
        heights = jax.random.uniform(jax.random.fold_in(jax.random.fold_in(key, 6), axis_at), (shards_of,), jnp.float32, low / len(cuts), high / len(cuts))
        gain = gain * jnp.repeat(jnp.exp(heights), shape[axis_at] // shards_of).reshape((-1,) + (1,) * (len(shape) - 1 - axis_at))
    return gain


def scatter_about(key, extent, scale, bound, cuts=(), kind=jnp.bfloat16):
    entries = scale * jax.random.normal(key, extent, jnp.float32)
    if cuts:
        entries = entries * level_of(key, extent, cuts, -0.22, 0.18)
    return jnp.clip(entries, -bound, bound).astype(kind)


def setup_inputs(seed: int = 0) -> dict:
    key_of = jax.random.split(jax.random.key(seed), 9)
    return {
        "features": scatter_about(key_of[0], (VOXELS, C1), 1.0, 6.0, ((0, 128),)),
        "conv_weight": scatter_about(key_of[1], (27, C1, C1), (14 * C1) ** -0.5, 0.125),
        "down_weight": scatter_about(key_of[2], (8, C1, C2), (4 * C1) ** -0.5, 0.25),
        "neighbour_map": draw_neighbour_map(jax.random.fold_in(key_of[8], 71), 0),
        "halo_rows": draw_halo_rows(jax.random.fold_in(key_of[8], 71), 0),
        "child_map": draw_child_map(jax.random.fold_in(key_of[8], 71), 0),
        "child_rows": draw_child_rows(jax.random.fold_in(key_of[8], 71), 0),
        "out_grad": scatter_about(key_of[7], (PARENTS, C2), 1.0, 6.0, ((0, 128),)),
    }


def offsets_list(slot_count):
    half_count = slot_count // 2
    return [number - half_count for number in range(half_count)] + [number + 1 for number in range(half_count)]

def conv_forward(extended, neighbours, weights):

    def accumulate(running, inputs):
        index_row, kernel = inputs
        picked = jnp.take(extended, index_row, axis=0)
        return (running + jnp.dot(picked, kernel, preferred_element_type=jnp.float32), None)
    start_sum = jnp.zeros((neighbours.shape[1], weights.shape[2]), jnp.float32)
    result, unused = lax.scan(accumulate, start_sum, (neighbours, weights))
    return result

def conv_backward(extended, neighbours, weights, upstream):

    def accumulate(carried, inputs):
        index_row, kernel = inputs
        picked = jnp.take(extended, index_row, axis=0)
        weight_grad = lax.dot_general(picked, upstream, (((0,), (0,)), ((), ())), preferred_element_type=jnp.float32)
        back_rows = lax.dot_general(upstream, kernel, (((1,), (1,)), ((), ())), preferred_element_type=jnp.float32)
        return (carried.at[index_row].add(back_rows), weight_grad)
    start_sum = jnp.zeros((extended.shape[0], extended.shape[1]), jnp.float32)
    return lax.scan(accumulate, start_sum, (neighbours, weights))

def silu_slope(values):
    sigmoid_value = jax.nn.sigmoid(values)
    return sigmoid_value * (1.0 + values * (1.0 - sigmoid_value))

def incoming_rows(padded_all, rows_all, device, offsets):
    pieces = []
    for number in range(len(offsets)):
        source = device - offsets[number]
        in_range = (source >= 0) & (source < N_SHARD)
        clipped = jnp.clip(source, 0, N_SHARD - 1).astype(jnp.int32)
        source_table = lax.dynamic_index_in_dim(padded_all, clipped, 0, keepdims=False)
        wanted = lax.dynamic_index_in_dim(rows_all, clipped, 0, keepdims=False)[number]
        taken_rows = jnp.take(source_table, wanted, axis=0)
        pieces.append(jnp.where(in_range, taken_rows, jnp.zeros_like(taken_rows)))
    return jnp.concatenate(pieces)

def returned_rows(back_all, rows_all, device, offsets):
    gathered_sum = jnp.zeros((V_DEV + 1, back_all.shape[-1]), jnp.float32)
    own_rows = lax.dynamic_index_in_dim(rows_all, device, 0, keepdims=False)
    for number in range(len(offsets)):
        target = device + offsets[number]
        in_range = (target >= 0) & (target < N_SHARD)
        clipped = jnp.clip(target, 0, N_SHARD - 1).astype(jnp.int32)
        returned = lax.dynamic_index_in_dim(back_all, clipped, 0, keepdims=False)[number]
        returned = jnp.where(in_range, returned, jnp.zeros_like(returned))
        gathered_sum = gathered_sum.at[own_rows[number]].add(returned)
    return gathered_sum[:V_DEV]

def reference(features, conv_weight, down_weight, neighbour_map, halo_rows, child_map, child_rows, out_grad):
    offsets = offsets_list(SLOTS)
    device_ids = jnp.arange(N_SHARD, dtype=jnp.int32)
    feats_all = features.reshape(N_SHARD, V_DEV, C1)
    padded_x = jnp.concatenate([feats_all, jnp.zeros((N_SHARD, 1, C1), features.dtype)], axis=1)
    maps_x = neighbour_map.reshape(27, N_SHARD, V_DEV).transpose(1, 0, 2)
    lists_x = halo_rows.reshape(SLOTS, N_SHARD, CAP).transpose(1, 0, 2)
    maps_h = child_map.reshape(8, N_SHARD, P_DEV).transpose(1, 0, 2)
    lists_h = child_rows.reshape(SLOTS, N_SHARD, CAP2).transpose(1, 0, 2)
    grads_all = out_grad.reshape(N_SHARD, P_DEV, C2)
    zero_row = jnp.zeros((1, C1), features.dtype)

    def extended_x(device):
        return jnp.concatenate([feats_all[device], incoming_rows(padded_x, lists_x, device, offsets), zero_row])

    def forward_one(device):
        pre_act = conv_forward(extended_x(device), maps_x[device], conv_weight)
        hidden = (feats_all[device].astype(jnp.float32) + jax.nn.silu(pre_act)).astype(jnp.bfloat16)
        return (pre_act, hidden)
    pre_all, hidden_all = lax.map(forward_one, device_ids)
    padded_h = jnp.concatenate([hidden_all, jnp.zeros((N_SHARD, 1, C1), jnp.bfloat16)], axis=1)

    def down_one(device):
        extended = jnp.concatenate([hidden_all[device], incoming_rows(padded_h, lists_h, device, offsets), zero_row])
        lowered = conv_forward(extended, maps_h[device], down_weight).astype(jnp.bfloat16)
        back_ext, weight_terms = conv_backward(extended, maps_h[device], down_weight, grads_all[device])
        return (lowered, back_ext, weight_terms)
    lowered_all, back_h_all, down_terms = lax.map(down_one, device_ids)
    back_h_slots = back_h_all[:, V_DEV:V_DEV + SLOTS * CAP2].reshape(N_SHARD, SLOTS, CAP2, C1)

    def middle_one(device):
        hidden_grad = back_h_all[device, :V_DEV] + returned_rows(back_h_slots, lists_h, device, offsets)
        pre_grad = (hidden_grad * silu_slope(pre_all[device])).astype(jnp.bfloat16)
        back_ext, weight_terms = conv_backward(extended_x(device), maps_x[device], conv_weight, pre_grad)
        return (hidden_grad, back_ext, weight_terms)
    hidden_grads, back_x_all, conv_terms = lax.map(middle_one, device_ids)
    back_x_slots = back_x_all[:, V_DEV:V_DEV + SLOTS * CAP].reshape(N_SHARD, SLOTS, CAP, C1)

    def final_one(device):
        return hidden_grads[device] + back_x_all[device, :V_DEV] + returned_rows(back_x_slots, lists_x, device, offsets)
    input_grad = lax.map(final_one, device_ids).reshape(VOXELS, C1)
    grad_scale = 1.0 / math.sqrt(VOXELS)
    return (lowered_all.reshape(PARENTS, C2), input_grad, lax.optimization_barrier(jnp.sum(conv_terms, axis=0)) * grad_scale, lax.optimization_barrier(jnp.sum(down_terms, axis=0)) * grad_scale)
```

```python
import math

import jax
import jax.numpy as jnp
from jax import lax
from jax.experimental import pallas as pl
from jax.experimental.pallas import tpu as pltpu
from jax.sharding import PartitionSpec as P

MESH = pl.DeviceIdType.MESH
BF = jnp.bfloat16
F32 = jnp.float32
K = 27
O = 8
V = 1024
PD = 256
C = 128
C2 = 256
S = 4
CAP = 64
CAP2 = 32
HALF = V // 2
PAIRS = HALF + 128
OFFSETS = (-2, -1, 1, 2)


def row_codes(rows, last, fold_received):
    received = rows >= V
    in_received = (rows >> 7) & 1 if fold_received else jnp.zeros_like(rows)
    side = jnp.where(received, in_received, (rows >> 9) & 1)
    block = jnp.where(received, 4, (rows >> 7) & 3)
    code = ((rows & 127) + 128) << block
    code = jnp.where(side == 1, -code, code)
    return jnp.where(rows >= last, 0, code).astype(F32)


def table_codes(shape, dim, start=0):
    place = lax.broadcasted_iota(jnp.int32, shape, dim) + start
    return (((place & 127) + 128) << (place >> 7)).astype(F32).astype(BF)


def pick_matrix(codes):
    size = jnp.abs(codes)
    names = table_codes((1, PAIRS), 1)
    one, zero = jnp.ones((), BF), jnp.zeros((), BF)
    return jnp.concatenate(
        [jnp.where(size == names[:, b * 128 : (b + 1) * 128], one, zero) for b in range(PAIRS // 128)], axis=1
    )


def spread_matrix(row, start, count):
    n = row.shape[1]
    size = jnp.broadcast_to(jnp.abs(row), (count, n)).astype(BF)
    names = table_codes((count, 128), 0, start)
    names = jnp.concatenate([names] * (n // 128), axis=1)
    return jnp.where(size == names, jnp.ones((), BF), jnp.zeros((), BF))


def pick_side(both, codes):
    both = both.astype(BF)
    return jnp.where(codes < 0, both[:, C:], both[:, :C])


def two_sides(rows, codes):
    zero = jnp.zeros((), BF)
    return jnp.concatenate([jnp.where(codes >= 0, rows, zero), jnp.where(codes < 0, rows, zero)], axis=1)


def dot(a, b):
    return jnp.dot(a, b, preferred_element_type=F32)


def dot_t(a, b):
    return lax.dot_general(a, b, (((1,), (1,)), ((), ())), preferred_element_type=F32)


def t_dot(a, b):
    return lax.dot_general(a, b, (((0,), (0,)), ((), ())), preferred_element_type=F32)


def list_matrix(lists, cap):
    row = jnp.concatenate([lists[s : s + 1, :] for s in range(S)], axis=1)
    places = lax.broadcasted_iota(jnp.int32, (V, S * cap), 0)
    return (places == row).astype(F32).astype(BF)


def kernel(
    features, conv_weight, down_weight, neighbour_map, halo_rows, child_map, child_rows, out_grad,
    coarse, input_grad, conv_terms, down_terms,
    codes_x, wide_x, codes_h, wide_h, picked, table, pre, hidden, hidden_grad, pre_grad, z_all, back_x, back_h,
    out_x, in_x, out_h, in_h, out_gh, in_gh, out_gx, in_gx, send_sem, recv_sem,
):
    n = lax.axis_size("shard")
    me = lax.axis_index("shard")

    def device(by):
        return (lax.rem(me + by + n, n),)

    barrier = pltpu.get_barrier_semaphore()
    for by in OFFSETS:
        pl.semaphore_signal(barrier, inc=1, device_id=device(by), device_id_type=MESH)

    def copies(which, src, dst, sign):
        return [
            pltpu.make_async_remote_copy(
                src_ref=src.at[s],
                dst_ref=dst.at[s],
                send_sem=send_sem.at[which, s],
                recv_sem=recv_sem.at[which, s],
                device_id=device(sign * OFFSETS[s]),
                device_id_type=MESH,
            )
            for s in range(S)
        ]

    chosen = t_dot(list_matrix(halo_rows[...], CAP), features[...]).astype(BF)
    for s in range(S):
        out_x[s] = chosen[s * CAP : (s + 1) * CAP]
    pl.semaphore_wait(barrier, S)
    send_x = copies(0, out_x, in_x, 1)
    for copy in send_x:
        copy.start()

    codes_h[...] = row_codes(child_map[...], V + S * CAP2, False)
    codes_turned = [codes_h[:, b * 128 : (b + 1) * 128].T for b in range(PD // 128)]
    for o in range(O):
        for b in range(PD // 128):
            wide_h[pl.ds(o * PD + b * 128, 128), :] = jnp.broadcast_to(codes_turned[b][:, o : o + 1], (128, 128)).astype(BF)
    for o in range(O):
        z = dot_t(out_grad[...], down_weight[o]).astype(BF)
        z_all[o, 0:PD, :] = two_sides(z, wide_h[pl.ds(o * PD, PD), :])
    total = jnp.zeros((PAIRS, 2 * C), F32)
    for o in range(O):
        total += dot(spread_matrix(codes_h[o : o + 1, :], 0, PAIRS), z_all[o, 0:PD, :])
    back_h[...] = total
    for s in range(S):
        out_gh[s] = back_h[pl.ds(HALF + s * CAP2, CAP2), 0:C].astype(BF)
    send_gh = copies(1, out_gh, in_gh, -1)
    for copy in send_gh:
        copy.start()

    codes_x[0:K, :] = row_codes(neighbour_map[...], V + S * CAP, True)
    codes_x[K:32, :] = jnp.zeros((32 - K, V), F32)

    def widen(b, carry):
        at = pl.ds(pl.multiple_of(b * 128, 128), 128)
        turned = codes_x[:, at].T
        for k in range(K):
            wide_x[k, at, :] = jnp.broadcast_to(turned[:, k : k + 1], (128, 128)).astype(BF)
        return carry

    lax.fori_loop(0, V // 128, widen, 0)

    table[0:HALF, 0:C] = features[0:HALF, :]
    table[0:HALF, C : 2 * C] = features[HALF:V, :]
    for copy in send_x:
        copy.wait_recv()
    for s in range(S):
        table[pl.ds(HALF + (s % 2) * CAP, CAP), pl.ds((s // 2) * C, C)] = in_x[s]
    pre[...] = jnp.zeros_like(pre)

    def forward(k, carry):
        codes = wide_x[k]
        rows = pick_side(dot(pick_matrix(codes), table[...]), codes)
        picked[k] = rows
        pre[...] += dot(rows, conv_weight[k])
        return carry

    lax.fori_loop(0, K, forward, 0)

    act = pre[...]
    gate = jax.nn.sigmoid(act)
    hidden[...] = (features[...].astype(F32) + act * gate).astype(BF)
    child_pick = list_matrix(child_rows[...], CAP2)
    chosen = t_dot(child_pick, hidden[...]).astype(BF)
    for s in range(S):
        out_h[s] = chosen[s * CAP2 : (s + 1) * CAP2]
    send_h = copies(2, out_h, in_h, 1)
    for copy in send_h:
        copy.start()
    for copy in send_gh:
        copy.wait_recv()
    returned = dot(child_pick, jnp.concatenate([in_gh[s] for s in range(S)], axis=0))
    grad_h = jnp.concatenate([back_h[0:HALF, 0:C], back_h[0:HALF, C : 2 * C]], axis=0) + returned
    hidden_grad[...] = grad_h
    pre_grad[...] = (grad_h * (gate * (1.0 + act * (1.0 - gate)))).astype(BF)

    turned_grad = pre_grad[...].T
    for k in range(0, K, 2):
        count = min(2, K - k)
        terms = dot(turned_grad, jnp.concatenate([picked[k + i] for i in range(count)], axis=1))
        for i in range(count):
            conv_terms[k + i] = terms[:, i * C : (i + 1) * C].T

    back_x[...] = jnp.zeros_like(back_x)

    def backward(k, carry):
        z = dot_t(pre_grad[...], conv_weight[k]).astype(BF)
        z_all[k] = two_sides(z, wide_x[k])
        row = codes_x[pl.ds(k, 1), :]
        back_x[HALF:PAIRS, :] += dot(spread_matrix(row, HALF, 128), z_all[k])
        return carry

    lax.fori_loop(0, K, backward, 0)
    for s in range(S):
        out_gx[s] = back_x[pl.ds(HALF + (s % 2) * CAP, CAP), pl.ds((s // 2) * C, C)].astype(BF)
    send_gx = copies(3, out_gx, in_gx, -1)
    for copy in send_gx:
        copy.start()

    def backward_local(k, carry):
        row = codes_x[pl.ds(k, 1), :]
        back_x[0:HALF, :] += dot(spread_matrix(row, 0, HALF), z_all[k])
        return carry

    lax.fori_loop(0, K, backward_local, 0)

    table[0:HALF, 0:C] = hidden[0:HALF, :]
    table[0:HALF, C : 2 * C] = hidden[HALF:V, :]
    table[HALF:PAIRS, C : 2 * C] = jnp.zeros((128, C), BF)
    for copy in send_h:
        copy.wait_recv()
    for s in range(S):
        table[pl.ds(HALF + s * CAP2, CAP2), 0:C] = in_h[s]
    total = jnp.zeros((PD, C2), F32)
    for o in range(O):
        codes = wide_h[pl.ds(o * PD, PD), :]
        rows = pick_side(dot(pick_matrix(codes), table[...]), codes)
        total += dot(rows, down_weight[o])
        down_terms[o] = t_dot(rows, out_grad[...])
    coarse[...] = total.astype(BF)

    for copy in send_gx:
        copy.wait_recv()
    returned = dot(list_matrix(halo_rows[...], CAP), jnp.concatenate([in_gx[s] for s in range(S)], axis=0))
    local_back = jnp.concatenate([back_x[0:HALF, 0:C], back_x[0:HALF, C : 2 * C]], axis=0)
    input_grad[...] = hidden_grad[...] + local_back + returned

    for copy in send_x + send_gh + send_h + send_gx:
        copy.wait_send()


def local(features, conv_weight, down_weight, neighbour_map, halo_rows, child_map, child_rows, out_grad):
    devices = lax.axis_size("shard")
    coarse, input_grad, conv_terms, down_terms = pl.pallas_call(
        kernel,
        out_shape=(
            jax.ShapeDtypeStruct((PD, C2), BF),
            jax.ShapeDtypeStruct((V, C), F32),
            jax.ShapeDtypeStruct((K, C, C), F32),
            jax.ShapeDtypeStruct((O, C, C2), F32),
        ),
        scratch_shapes=[
            pltpu.VMEM((32, V), F32),
            pltpu.VMEM((K, V, 128), BF),
            pltpu.VMEM((O, PD), F32),
            pltpu.VMEM((O * PD, 128), BF),
            pltpu.VMEM((K, V, C), BF),
            pltpu.VMEM((PAIRS, 2 * C), BF),
            pltpu.VMEM((V, C), F32),
            pltpu.VMEM((V, C), BF),
            pltpu.VMEM((V, C), F32),
            pltpu.VMEM((V, C), BF),
            pltpu.VMEM((K, V, 2 * C), BF),
            pltpu.VMEM((PAIRS, 2 * C), F32),
            pltpu.VMEM((PAIRS, 2 * C), F32),
            pltpu.VMEM((S, CAP, C), BF),
            pltpu.VMEM((S, CAP, C), BF),
            pltpu.VMEM((S, CAP2, C), BF),
            pltpu.VMEM((S, CAP2, C), BF),
            pltpu.VMEM((S, CAP2, C), BF),
            pltpu.VMEM((S, CAP2, C), BF),
            pltpu.VMEM((S, CAP, C), BF),
            pltpu.VMEM((S, CAP, C), BF),
            pltpu.SemaphoreType.DMA((4, S)),
            pltpu.SemaphoreType.DMA((4, S)),
        ],
        compiler_params=pltpu.CompilerParams(
            collective_id=0, has_side_effects=True, vmem_limit_bytes=56 * 2**20
        ),
    )(features, conv_weight, down_weight, neighbour_map, halo_rows, child_map, child_rows, out_grad)
    conv_summed, down_summed = lax.psum((conv_terms, down_terms), "shard")
    grad_scale = 1.0 / math.sqrt(V * devices)
    return (coarse, input_grad, conv_summed * grad_scale, down_summed * grad_scale)


def solution(mesh):
    return jax.shard_map(
        local,
        mesh=mesh,
        in_specs=(
            P("shard", None),
            P(),
            P(),
            P(None, "shard"),
            P(None, "shard"),
            P(None, "shard"),
            P(None, "shard"),
            P("shard", None),
        ),
        out_specs=(P("shard", None), P("shard", None), P(), P()),
        check_vma=False,
    )
```

```python
import math

import jax
import jax.numpy as jnp
from jax import lax
from jax.experimental import pallas as pl
from jax.experimental.pallas import tpu as pltpu
from jax.sharding import PartitionSpec as P

MESH = pl.DeviceIdType.MESH
BF = jnp.bfloat16
F32 = jnp.float32
K = 27
O = 8
V = 1024
PD = 256
C = 128
C2 = 256
S = 4
CAP = 64
CAP2 = 32
HALF = V // 2
PAIRS = HALF + 128
OFFSETS = (-2, -1, 1, 2)
AXES = ((2, 8, 32), (8, 32, 2), (32, 2, 8))


def row_codes(rows, last, fold_received):
    received = rows >= V
    in_received = (rows >> 7) & 1 if fold_received else jnp.zeros_like(rows)
    side = jnp.where(received, in_received, (rows >> 9) & 1)
    block = jnp.where(received, 4, (rows >> 7) & 3)
    code = ((rows & 127) + 128) << block
    code = jnp.where(side == 1, -code, code)
    return jnp.where(rows >= last, 0, code).astype(F32)


def table_codes(shape, dim, start=0):
    place = lax.broadcasted_iota(jnp.int32, shape, dim) + start
    return (((place & 127) + 128) << (place >> 7)).astype(F32).astype(BF)


def pick_matrix(codes):
    size = jnp.abs(codes)
    names = table_codes((1, PAIRS), 1)
    one, zero = jnp.ones((), BF), jnp.zeros((), BF)
    return jnp.concatenate(
        [jnp.where(size == names[:, b * 128 : (b + 1) * 128], one, zero) for b in range(PAIRS // 128)], axis=1
    )


def spread_matrix(row, start, count):
    n = row.shape[1]
    size = jnp.broadcast_to(jnp.abs(row), (count, n)).astype(BF)
    names = table_codes((count, 128), 0, start)
    names = jnp.concatenate([names] * (n // 128), axis=1)
    return jnp.where(size == names, jnp.ones((), BF), jnp.zeros((), BF))


def pick_side(both, codes):
    both = both.astype(BF)
    return jnp.where(codes < 0, both[:, C:], both[:, :C])


def two_sides(rows, codes):
    zero = jnp.zeros((), BF)
    return jnp.concatenate([jnp.where(codes >= 0, rows, zero), jnp.where(codes < 0, rows, zero)], axis=1)


def dot(a, b):
    return jnp.dot(a, b, preferred_element_type=F32)


def dot_t(a, b):
    return lax.dot_general(a, b, (((1,), (1,)), ((), ())), preferred_element_type=F32)


def t_dot(a, b):
    return lax.dot_general(a, b, (((0,), (0,)), ((), ())), preferred_element_type=F32)


def list_matrix(lists, cap):
    row = jnp.concatenate([lists[s : s + 1, :] for s in range(S)], axis=1)
    places = lax.broadcasted_iota(jnp.int32, (V, S * cap), 0)
    return (places == row).astype(F32).astype(BF)


def kernel(
    features, conv_weight, down_weight, neighbour_map, halo_rows, child_map, child_rows, out_grad,
    coarse, input_grad, summed,
    codes_x, wide_x, codes_h, wide_h, picked, table, pre, hidden, hidden_grad, pre_grad, z_all, back_x, back_h,
    out_x, in_x, out_h, in_h, out_gh, in_gh, out_gx, in_gx, send_sem, recv_sem,
    terms, got_core, sum_1, got_1, sum_2, got_2, sum_3, got_3, sum_send, sum_recv,
):
    n = lax.axis_size("shard")
    me = lax.axis_index("shard")
    core = lax.rem(me, 2)
    place = {stride: lax.rem(me // stride, 4) for stride in (2, 8, 32)}

    def along(stride, by):
        return me + (lax.rem(place[stride] + by, 4) - place[stride]) * stride

    def device(by):
        return (lax.rem(me + by + n, n),)

    barrier = pltpu.get_barrier_semaphore()
    for by in OFFSETS:
        pl.semaphore_signal(barrier, inc=1, device_id=device(by), device_id_type=MESH)
    sibling = me + 1 - 2 * core
    pl.semaphore_signal(barrier, inc=1, device_id=(sibling,), device_id_type=MESH)
    for stride in (2, 8, 32):
        for by in (1, 2, 3):
            pl.semaphore_signal(barrier, inc=1, device_id=(along(stride, by),), device_id_type=MESH)

    def copies(which, src, dst, sign):
        return [
            pltpu.make_async_remote_copy(
                src_ref=src.at[s],
                dst_ref=dst.at[s],
                send_sem=send_sem.at[which, s],
                recv_sem=recv_sem.at[which, s],
                device_id=device(sign * OFFSETS[s]),
                device_id_type=MESH,
            )
            for s in range(S)
        ]

    def remote(src, dst, step, part, lane, to):
        return pltpu.make_async_remote_copy(
            src_ref=src,
            dst_ref=dst,
            send_sem=sum_send.at[step, part, lane],
            recv_sem=sum_recv.at[step, part, lane],
            device_id=(to,),
            device_id_type=MESH,
        )

    held = ((sum_1, got_1, 256), (sum_2, got_2, 64), (sum_3, got_3, 16))
    flying = []

    def spread_step(level, part):
        stride = AXES[part][level]
        source, landing, _ = held[level]
        return [
            remote(
                source.at[part, lax.rem(place[stride] + by, 4)], landing.at[part, by - 1], 1 + level, part, by - 1, along(stride, by)
            )
            for by in (1, 2, 3)
        ]

    def start_all(moves):
        for move in moves:
            move.start()
        flying.extend(moves)
        return moves

    def reduce_start(part):
        return start_all([remote(terms.at[part, 1 - core], got_core.at[part], 0, part, 0, sibling)])

    def reduce_core(part, moves):
        for move in moves:
            move.wait_recv()
        total = (terms[part, core].astype(F32) + got_core[part].astype(F32)).astype(BF)
        for q in range(4):
            sum_1[part, q] = total[q * 256 : (q + 1) * 256]
        return start_all(spread_step(0, part))

    def reduce_axis(level, part, moves):
        for move in moves:
            move.wait_recv()
        source, landing, _ = held[level]
        total = source[part, place[AXES[part][level]]].astype(F32)
        for by in range(3):
            total += landing[part, by].astype(F32)
        total = total.astype(BF)
        if level < 2:
            target, _, rows = held[level + 1]
            for q in range(4):
                target[part, q] = total[q * rows : (q + 1) * rows]
            return start_all(spread_step(level + 1, part))
        summed[part, mine(part, 3), :] = total
        return gather_step(2, part)

    def mine(part, depth):
        start, size = core * 1024, 1024
        for level in range(depth):
            size = size // 4
            start = start + place[AXES[part][level]] * size
        return pl.ds(pl.multiple_of(start, 16), size)

    def gather_step(level, part):
        rows = mine(part, level + 1)
        return start_all(
            [
                remote(summed.at[part, rows], summed.at[part, rows], 6 - level, part, by - 1, along(AXES[part][level], by))
                for by in (1, 2, 3)
            ]
        )

    def gather_axis(level, part, moves):
        for move in moves:
            move.wait_recv()
        if level > 0:
            return gather_step(level - 1, part)
        rows = mine(part, 0)
        return start_all([remote(summed.at[part, rows], summed.at[part, rows], 7, part, 0, sibling)])

    sums = [None] * 3

    def sum_turn(turn):
        for part in range(3):
            if turn == 0:
                sums[part] = reduce_core(part, sums[part])
            elif turn <= 3:
                sums[part] = reduce_axis(turn - 1, part, sums[part])
            else:
                sums[part] = gather_axis(6 - turn, part, sums[part])

    chosen = t_dot(list_matrix(halo_rows[...], CAP), features[...]).astype(BF)
    for s in range(S):
        out_x[s] = chosen[s * CAP : (s + 1) * CAP]
    pl.semaphore_wait(barrier, S + 10)
    send_x = copies(0, out_x, in_x, 1)
    for copy in send_x:
        copy.start()

    codes_h[...] = row_codes(child_map[...], V + S * CAP2, False)
    codes_turned = [codes_h[:, b * 128 : (b + 1) * 128].T for b in range(PD // 128)]
    for o in range(O):
        for b in range(PD // 128):
            wide_h[pl.ds(o * PD + b * 128, 128), :] = jnp.broadcast_to(codes_turned[b][:, o : o + 1], (128, 128)).astype(BF)
    for o in range(O):
        z = dot_t(out_grad[...], down_weight[o]).astype(BF)
        z_all[o, 0:PD, :] = two_sides(z, wide_h[pl.ds(o * PD, PD), :])
    total = jnp.zeros((PAIRS, 2 * C), F32)
    for o in range(O):
        total += dot(spread_matrix(codes_h[o : o + 1, :], 0, PAIRS), z_all[o, 0:PD, :])
    back_h[...] = total
    for s in range(S):
        out_gh[s] = back_h[pl.ds(HALF + s * CAP2, CAP2), 0:C].astype(BF)
    send_gh = copies(1, out_gh, in_gh, -1)
    for copy in send_gh:
        copy.start()

    codes_x[0:K, :] = row_codes(neighbour_map[...], V + S * CAP, True)
    codes_x[K:32, :] = jnp.zeros((32 - K, V), F32)

    def widen(b, carry):
        at = pl.ds(pl.multiple_of(b * 128, 128), 128)
        turned = codes_x[:, at].T
        for k in range(K):
            wide_x[k, at, :] = jnp.broadcast_to(turned[:, k : k + 1], (128, 128)).astype(BF)
        return carry

    lax.fori_loop(0, V // 128, widen, 0)

    table[0:HALF, 0:C] = features[0:HALF, :]
    table[0:HALF, C : 2 * C] = features[HALF:V, :]
    for copy in send_x:
        copy.wait_recv()
    for s in range(S):
        table[pl.ds(HALF + (s % 2) * CAP, CAP), pl.ds((s // 2) * C, C)] = in_x[s]
    pre[...] = jnp.zeros_like(pre)

    def forward(k, carry):
        codes = wide_x[k]
        rows = pick_side(dot(pick_matrix(codes), table[...]), codes)
        picked[k] = rows
        pre[...] += dot(rows, conv_weight[k])
        return carry

    lax.fori_loop(0, K, forward, 0)

    act = pre[...]
    gate = jax.nn.sigmoid(act)
    hidden[...] = (features[...].astype(F32) + act * gate).astype(BF)
    child_pick = list_matrix(child_rows[...], CAP2)
    chosen = t_dot(child_pick, hidden[...]).astype(BF)
    for s in range(S):
        out_h[s] = chosen[s * CAP2 : (s + 1) * CAP2]
    send_h = copies(2, out_h, in_h, 1)
    for copy in send_h:
        copy.start()
    for copy in send_gh:
        copy.wait_recv()
    returned = dot(child_pick, jnp.concatenate([in_gh[s] for s in range(S)], axis=0))
    grad_h = jnp.concatenate([back_h[0:HALF, 0:C], back_h[0:HALF, C : 2 * C]], axis=0) + returned
    hidden_grad[...] = grad_h
    pre_grad[...] = (grad_h * (gate * (1.0 + act * (1.0 - gate)))).astype(BF)

    turned_grad = pre_grad[...].T
    for k in range(0, K, 2):
        count = min(2, K - k)
        products = dot(turned_grad, jnp.concatenate([picked[k + i] for i in range(count)], axis=1))
        for i in range(count):
            block = k + i
            terms[block // 16, (block // 8) % 2, pl.ds(block % 8 * C, C), :] = products[:, i * C : (i + 1) * C].T.astype(BF)
    for block in range(K, 32):
        terms[block // 16, (block // 8) % 2, pl.ds(block % 8 * C, C), :] = jnp.zeros((C, C), BF)
    sums[0] = reduce_start(0)
    sums[1] = reduce_start(1)

    table[0:HALF, 0:C] = hidden[0:HALF, :]
    table[0:HALF, C : 2 * C] = hidden[HALF:V, :]
    table[HALF:PAIRS, C : 2 * C] = jnp.zeros((128, C), BF)
    for copy in send_h:
        copy.wait_recv()
    for s in range(S):
        table[pl.ds(HALF + s * CAP2, CAP2), 0:C] = in_h[s]
    total = jnp.zeros((PD, C2), F32)
    for o in range(O):
        codes = wide_h[pl.ds(o * PD, PD), :]
        rows = pick_side(dot(pick_matrix(codes), table[...]), codes)
        total += dot(rows, down_weight[o])
        products = t_dot(rows, out_grad[...]).astype(BF)
        terms[2, o // 4, pl.ds(o % 4 * 2 * C, C), :] = products[:, 0:C]
        terms[2, o // 4, pl.ds((o % 4 * 2 + 1) * C, C), :] = products[:, C : 2 * C]
    coarse[...] = total.astype(BF)

    sums[2] = reduce_start(2)

    back_x[...] = jnp.zeros_like(back_x)

    def backward(k, carry):
        z = dot_t(pre_grad[...], conv_weight[k]).astype(BF)
        z_all[k] = two_sides(z, wide_x[k])
        row = codes_x[pl.ds(k, 1), :]
        back_x[HALF:PAIRS, :] += dot(spread_matrix(row, HALF, 128), z_all[k])
        return carry

    lax.fori_loop(0, 9, backward, 0)
    sum_turn(0)
    lax.fori_loop(9, K, backward, 0)
    sum_turn(1)
    for s in range(S):
        out_gx[s] = back_x[pl.ds(HALF + (s % 2) * CAP, CAP), pl.ds((s // 2) * C, C)].astype(BF)
    send_gx = copies(3, out_gx, in_gx, -1)
    for copy in send_gx:
        copy.start()

    def backward_local(k, carry):
        row = codes_x[pl.ds(k, 1), :]
        back_x[0:HALF, :] += dot(spread_matrix(row, 0, HALF), z_all[k])
        return carry

    lax.fori_loop(0, 6, backward_local, 0)
    sum_turn(2)
    lax.fori_loop(6, 12, backward_local, 0)
    sum_turn(3)
    lax.fori_loop(12, 18, backward_local, 0)
    sum_turn(4)
    lax.fori_loop(18, K, backward_local, 0)
    sum_turn(5)

    for copy in send_gx:
        copy.wait_recv()
    returned = dot(list_matrix(halo_rows[...], CAP), jnp.concatenate([in_gx[s] for s in range(S)], axis=0))
    local_back = jnp.concatenate([back_x[0:HALF, 0:C], back_x[0:HALF, C : 2 * C]], axis=0)
    input_grad[...] = hidden_grad[...] + local_back + returned

    sum_turn(6)
    for part in range(3):
        for move in sums[part]:
            move.wait_recv()
    for copy in send_x + send_gh + send_h + send_gx + flying:
        copy.wait_send()


def local(features, conv_weight, down_weight, neighbour_map, halo_rows, child_map, child_rows, out_grad):
    devices = lax.axis_size("shard")
    coarse, input_grad, summed = pl.pallas_call(
        kernel,
        out_shape=(
            jax.ShapeDtypeStruct((PD, C2), BF),
            jax.ShapeDtypeStruct((V, C), F32),
            jax.ShapeDtypeStruct((3, 2048, C), BF),
        ),
        scratch_shapes=[
            pltpu.VMEM((32, V), F32),
            pltpu.VMEM((K, V, 128), BF),
            pltpu.VMEM((O, PD), F32),
            pltpu.VMEM((O * PD, 128), BF),
            pltpu.VMEM((K, V, C), BF),
            pltpu.VMEM((PAIRS, 2 * C), BF),
            pltpu.VMEM((V, C), F32),
            pltpu.VMEM((V, C), BF),
            pltpu.VMEM((V, C), F32),
            pltpu.VMEM((V, C), BF),
            pltpu.VMEM((K, V, 2 * C), BF),
            pltpu.VMEM((PAIRS, 2 * C), F32),
            pltpu.VMEM((PAIRS, 2 * C), F32),
            pltpu.VMEM((S, CAP, C), BF),
            pltpu.VMEM((S, CAP, C), BF),
            pltpu.VMEM((S, CAP2, C), BF),
            pltpu.VMEM((S, CAP2, C), BF),
            pltpu.VMEM((S, CAP2, C), BF),
            pltpu.VMEM((S, CAP2, C), BF),
            pltpu.VMEM((S, CAP, C), BF),
            pltpu.VMEM((S, CAP, C), BF),
            pltpu.SemaphoreType.DMA((4, S)),
            pltpu.SemaphoreType.DMA((4, S)),
            pltpu.VMEM((3, 2, 1024, C), BF),
            pltpu.VMEM((3, 1024, C), BF),
            pltpu.VMEM((3, 4, 256, C), BF),
            pltpu.VMEM((3, 3, 256, C), BF),
            pltpu.VMEM((3, 4, 64, C), BF),
            pltpu.VMEM((3, 3, 64, C), BF),
            pltpu.VMEM((3, 4, 16, C), BF),
            pltpu.VMEM((3, 3, 16, C), BF),
            pltpu.SemaphoreType.DMA((8, 3, 3)),
            pltpu.SemaphoreType.DMA((8, 3, 3)),
        ],
        compiler_params=pltpu.CompilerParams(
            collective_id=0, has_side_effects=True, vmem_limit_bytes=56 * 2**20
        ),
    )(features, conv_weight, down_weight, neighbour_map, halo_rows, child_map, child_rows, out_grad)
    grad_scale = 1.0 / math.sqrt(V * devices)
    blocks = summed.reshape(48, C, C)
    conv_grad = blocks[:K].astype(F32) * grad_scale
    down_grad = blocks[32:].reshape(O, 2, C, C).transpose(0, 2, 1, 3).reshape(O, C, C2).astype(F32) * grad_scale
    return (coarse, input_grad, conv_grad, down_grad)


def solution(mesh):
    return jax.shard_map(
        local,
        mesh=mesh,
        in_specs=(
            P("shard", None),
            P(),
            P(),
            P(None, "shard"),
            P(None, "shard"),
            P(None, "shard"),
            P(None, "shard"),
            P("shard", None),
        ),
        out_specs=(P("shard", None), P("shard", None), P(), P()),
        check_vma=False,
    )
```

```python
import math

import jax
import jax.numpy as jnp
from jax import lax
from jax.experimental import pallas as pl
from jax.experimental.pallas import tpu as pltpu
from jax.sharding import PartitionSpec as P

MESH = pl.DeviceIdType.MESH
BF = jnp.bfloat16
F32 = jnp.float32
K = 27
O = 8
V = 1024
PD = 256
C = 128
C2 = 256
S = 4
CAP = 64
CAP2 = 32
HALF = V // 2
PAIRS = HALF + 128
OFFSETS = (-2, -1, 1, 2)
PLANES = ((2, 8, 32), (8, 32, 2), (32, 2, 8))
CHUNK = (64, 48, 64)
HOPS = [(i, j) for i in (2, 1, 3, 0) for j in (2, 1, 3, 0) if i or j]


def row_codes(rows, last, fold_received):
    received = rows >= V
    in_received = (rows >> 7) & 1 if fold_received else jnp.zeros_like(rows)
    side = jnp.where(received, in_received, (rows >> 9) & 1)
    block = jnp.where(received, 4, (rows >> 7) & 3)
    code = ((rows & 127) + 128) << block
    code = jnp.where(side == 1, -code, code)
    return jnp.where(rows >= last, 0, code).astype(F32)


def table_codes(shape, dim, start=0):
    place = lax.broadcasted_iota(jnp.int32, shape, dim) + start
    return (((place & 127) + 128) << (place >> 7)).astype(F32).astype(BF)


def pick_matrix(codes):
    size = jnp.abs(codes)
    names = table_codes((1, PAIRS), 1)
    one, zero = jnp.ones((), BF), jnp.zeros((), BF)
    return jnp.concatenate(
        [jnp.where(size == names[:, b * 128 : (b + 1) * 128], one, zero) for b in range(PAIRS // 128)], axis=1
    )


def spread_matrix(row, start, count):
    n = row.shape[1]
    size = jnp.broadcast_to(jnp.abs(row), (count, n)).astype(BF)
    names = table_codes((count, 128), 0, start)
    names = jnp.concatenate([names] * (n // 128), axis=1)
    return jnp.where(size == names, jnp.ones((), BF), jnp.zeros((), BF))


def pick_side(both, codes):
    both = both.astype(BF)
    return jnp.where(codes < 0, both[:, C:], both[:, :C])


def two_sides(rows, codes):
    zero = jnp.zeros((), BF)
    return jnp.concatenate([jnp.where(codes >= 0, rows, zero), jnp.where(codes < 0, rows, zero)], axis=1)


def dot(a, b):
    return jnp.dot(a, b, preferred_element_type=F32)


def dot_t(a, b):
    return lax.dot_general(a, b, (((1,), (1,)), ((), ())), preferred_element_type=F32)


def t_dot(a, b):
    return lax.dot_general(a, b, (((0,), (0,)), ((), ())), preferred_element_type=F32)


def list_matrix(lists, cap):
    row = jnp.concatenate([lists[s : s + 1, :] for s in range(S)], axis=1)
    places = lax.broadcasted_iota(jnp.int32, (V, S * cap), 0)
    return (places == row).astype(F32).astype(BF)


def kernel(
    features, conv_weight, down_weight, neighbour_map, halo_rows, child_map, child_rows, out_grad,
    coarse, input_grad, summed,
    codes_x, wide_x, codes_h, wide_h, picked, table, pre, hidden, hidden_grad, pre_grad, z_all, back_x, back_h,
    out_x, in_x, out_h, in_h, out_gh, in_gh, out_gx, in_gx, send_sem, recv_sem,
    terms, got_core, core_sum, got_plane, plane_sum,
    core_send, core_recv, plane_send, plane_recv, axis_send, axis_recv,
):
    n = lax.axis_size("shard")
    me = lax.axis_index("shard")
    core = lax.rem(me, 2)
    place = {stride: lax.rem(me // stride, 4) for stride in (2, 8, 32)}

    def shift(stride, by):
        return (lax.rem(place[stride] + by, 4) - place[stride]) * stride

    def device(by):
        return (lax.rem(me + by + n, n),)

    barrier = pltpu.get_barrier_semaphore()
    for by in OFFSETS:
        pl.semaphore_signal(barrier, inc=1, device_id=device(by), device_id_type=MESH)
    sibling = me + 1 - 2 * core
    pl.semaphore_signal(barrier, inc=1, device_id=(sibling,), device_id_type=MESH)
    for a, b, _ in PLANES:
        for i, j in HOPS:
            if i and j:
                to = me + shift(a, i) + shift(b, j)
                pl.semaphore_signal(barrier, inc=1, device_id=(to,), device_id_type=MESH)
        for i in (1, 2, 3):
            pl.semaphore_signal(barrier, inc=1, device_id=(me + shift(a, i),), device_id_type=MESH)

    def copies(which, src, dst, sign):
        return [
            pltpu.make_async_remote_copy(
                src_ref=src.at[s],
                dst_ref=dst.at[s],
                send_sem=send_sem.at[which, s],
                recv_sem=recv_sem.at[which, s],
                device_id=device(sign * OFFSETS[s]),
                device_id_type=MESH,
            )
            for s in range(S)
        ]

    flying = []

    def send(src, dst, sems, at, to):
        move = pltpu.make_async_remote_copy(
            src_ref=src,
            dst_ref=dst,
            send_sem=sems[0].at[at],
            recv_sem=sems[1].at[at],
            device_id=(to,),
            device_id_type=MESH,
        )
        return move

    def start_all(moves):
        for move in moves:
            move.start()
        flying.extend(moves)
        return moves

    core_sems, plane_sems, axis_sems = (core_send, core_recv), (plane_send, plane_recv), (axis_send, axis_recv)
    sums = [()] * 3

    def put_block(block, value):
        part = 0 if block < 16 else 1 if block < 28 else 2
        at = block - (0, 16, 28)[part]
        per_half = CHUNK[part] // 8
        terms[part, at // per_half, pl.ds(at % per_half * C, C), :] = value


    def sum_turn(turn, parts):
        for part in parts:
            for move in sums[part]:
                move.wait_recv()
            sums[part] = start_all(sum_step(turn, part))

    def sum_step(turn, part):
        a, b, c = PLANES[part]
        size = CHUNK[part]
        here = place[a] * 4 + place[b]
        half = pl.ds(0, 16 * size)
        chunk = pl.ds(0, size)
        owned = pl.ds(pl.multiple_of(core * (16 * size) + here * size, 16), size)
        if turn == 0:
            return [send(terms.at[part, 1 - core, half], got_core.at[part, half], core_sems, (0, part), sibling)]
        if turn == 1:
            total = (terms[part, core, half].astype(F32) + got_core[part, half].astype(F32)).astype(BF)
            for q in range(16):
                core_sum[part, q, chunk] = total[q * size : (q + 1) * size]
            return [
                send(
                    core_sum.at[part, lax.rem(place[a] + i, 4) * 4 + lax.rem(place[b] + j, 4), chunk],
                    got_plane.at[part, at, chunk], plane_sems, (0, part, at), me + shift(a, i) + shift(b, j),
                )
                for at, (i, j) in enumerate(HOPS)
            ]
        if turn == 2:
            total = core_sum[part, here, chunk].astype(F32)
            for at in range(15):
                total += got_plane[part, at, chunk].astype(F32)
            plane_sum[part, place[c], chunk] = total
            mine = plane_sum.at[part, place[c], chunk]
            return [send(mine, mine, axis_sems, (part, i - 1), me + shift(c, i)) for i in (1, 2, 3)]
        if turn == 3:
            total = plane_sum[part, 0, chunk] + plane_sum[part, 1, chunk]
            total += plane_sum[part, 2, chunk] + plane_sum[part, 3, chunk]
            summed[part, owned] = total.astype(BF)
            mine = summed.at[part, owned]
            return [
                send(mine, mine, plane_sems, (1, part, at), me + shift(a, i) + shift(b, j)) for at, (i, j) in enumerate(HOPS)
            ]
        if turn == 4:
            mine = summed.at[part, pl.ds(pl.multiple_of(core * (16 * size), 16), 16 * size)]
            return [send(mine, mine, core_sems, (1, part), sibling)]
        return []

    chosen = t_dot(list_matrix(halo_rows[...], CAP), features[...]).astype(BF)
    for s in range(S):
        out_x[s] = chosen[s * CAP : (s + 1) * CAP]
    codes_x[0:K, :] = row_codes(neighbour_map[...], V + S * CAP, True)
    codes_x[K:32, :] = jnp.zeros((32 - K, V), F32)

    def widen(b, carry):
        at = pl.ds(pl.multiple_of(b * 128, 128), 128)
        turned = codes_x[:, at].T
        for k in range(K):
            wide_x[k, at, :] = jnp.broadcast_to(turned[:, k : k + 1], (128, 128)).astype(BF)
        return carry

    lax.fori_loop(0, 6, widen, 0)

    pl.semaphore_wait(barrier, S + 37)
    send_x = copies(0, out_x, in_x, 1)
    for copy in send_x:
        copy.start()

    lax.fori_loop(6, V // 128, widen, 0)

    codes_h[...] = row_codes(child_map[...], V + S * CAP2, False)
    codes_turned = [codes_h[:, b * 128 : (b + 1) * 128].T for b in range(PD // 128)]
    for o in range(O):
        for b in range(PD // 128):
            wide_h[pl.ds(o * PD + b * 128, 128), :] = jnp.broadcast_to(codes_turned[b][:, o : o + 1], (128, 128)).astype(BF)
    for o in range(O):
        z = dot_t(out_grad[...], down_weight[o]).astype(BF)
        z_all[o, 0:PD, :] = two_sides(z, wide_h[pl.ds(o * PD, PD), :])
    total = jnp.zeros((PAIRS, 2 * C), F32)
    for o in range(O):
        total += dot(spread_matrix(codes_h[o : o + 1, :], 0, PAIRS), z_all[o, 0:PD, :])
    back_h[...] = total
    for s in range(S):
        out_gh[s] = back_h[pl.ds(HALF + s * CAP2, CAP2), 0:C].astype(BF)
    send_gh = copies(1, out_gh, in_gh, -1)
    for copy in send_gh:
        copy.start()

    table[0:HALF, 0:C] = features[0:HALF, :]
    table[0:HALF, C : 2 * C] = features[HALF:V, :]
    for copy in send_x:
        copy.wait_recv()
    for s in range(S):
        table[pl.ds(HALF + (s % 2) * CAP, CAP), pl.ds((s // 2) * C, C)] = in_x[s]
    pre[...] = jnp.zeros_like(pre)

    def forward(step, carry):
        k = step * 3
        group = []
        for i in range(3):
            codes = wide_x[k + i]
            rows = pick_side(dot(pick_matrix(codes), table[...]), codes)
            picked[k + i] = rows
            group.append(rows)
        weights = conv_weight[pl.ds(k, 3)].reshape(3 * C, C)
        pre[...] += dot(jnp.concatenate(group, axis=1), weights)
        return carry

    lax.fori_loop(0, K // 3, forward, 0)

    act = pre[...]
    gate = jax.nn.sigmoid(act)
    hidden[...] = (features[...].astype(F32) + act * gate).astype(BF)
    child_pick = list_matrix(child_rows[...], CAP2)
    chosen = t_dot(child_pick, hidden[...]).astype(BF)
    for s in range(S):
        out_h[s] = chosen[s * CAP2 : (s + 1) * CAP2]
    send_h = copies(2, out_h, in_h, 1)
    for copy in send_h:
        copy.start()
    for copy in send_gh:
        copy.wait_recv()
    returned = dot(child_pick, jnp.concatenate([in_gh[s] for s in range(S)], axis=0))
    grad_h = jnp.concatenate([back_h[0:HALF, 0:C], back_h[0:HALF, C : 2 * C]], axis=0) + returned
    hidden_grad[...] = grad_h
    pre_grad[...] = (grad_h * (gate * (1.0 + act * (1.0 - gate)))).astype(BF)

    turned_grad = pre_grad[...].T
    for k in range(0, K, 2):
        count = min(2, K - k)
        products = dot(turned_grad, jnp.concatenate([picked[k + i] for i in range(count)], axis=1))
        for i in range(count):
            put_block(k + i, products[:, i * C : (i + 1) * C].T.astype(BF))
    put_block(K, jnp.zeros((C, C), BF))
    sum_turn(0, (0, 1))

    back_x[...] = jnp.zeros_like(back_x)

    def backward(step, carry):
        k = step * 3
        z = dot_t(pre_grad[...], conv_weight[pl.ds(k, 3)].reshape(3 * C, C)).astype(BF)
        total = back_x[HALF:PAIRS, :]
        for i in range(3):
            z2 = two_sides(z[:, i * C : (i + 1) * C], wide_x[k + i])
            z_all[k + i] = z2
            total += dot(spread_matrix(codes_x[pl.ds(k + i, 1), :], HALF, 128), z2)
        back_x[HALF:PAIRS, :] = total
        return carry

    lax.fori_loop(0, 2, backward, 0)
    sum_turn(1, (0, 1))

    table[0:HALF, 0:C] = hidden[0:HALF, :]
    table[0:HALF, C : 2 * C] = hidden[HALF:V, :]
    table[HALF:PAIRS, C : 2 * C] = jnp.zeros((128, C), BF)
    for copy in send_h:
        copy.wait_recv()
    for s in range(S):
        table[pl.ds(HALF + s * CAP2, CAP2), 0:C] = in_h[s]
    total = jnp.zeros((PD, C2), F32)
    for o in range(O):
        codes = wide_h[pl.ds(o * PD, PD), :]
        rows = pick_side(dot(pick_matrix(codes), table[...]), codes)
        total += dot(rows, down_weight[o])
        products = t_dot(rows, out_grad[...]).astype(BF)
        put_block(28 + 2 * o, products[:, 0:C])
        put_block(29 + 2 * o, products[:, C : 2 * C])
    coarse[...] = total.astype(BF)

    sum_turn(0, (2,))

    lax.fori_loop(2, 4, backward, 0)
    sum_turn(1, (2,))
    lax.fori_loop(4, 7, backward, 0)
    sum_turn(2, (0, 1))
    lax.fori_loop(7, K // 3, backward, 0)
    for s in range(S):
        out_gx[s] = back_x[pl.ds(HALF + (s % 2) * CAP, CAP), pl.ds((s // 2) * C, C)].astype(BF)
    send_gx = copies(3, out_gx, in_gx, -1)
    for copy in send_gx:
        copy.start()

    def backward_local(step, carry):
        k = step * 3
        total = back_x[0:HALF, :]
        for i in range(3):
            total += dot(spread_matrix(codes_x[pl.ds(k + i, 1), :], 0, HALF), z_all[k + i])
        back_x[0:HALF, :] = total
        return carry

    lax.fori_loop(0, 2, backward_local, 0)
    sum_turn(3, (0, 1))
    sum_turn(2, (2,))
    lax.fori_loop(2, 5, backward_local, 0)
    sum_turn(3, (2,))
    lax.fori_loop(5, K // 3, backward_local, 0)
    sum_turn(4, (0, 1))

    for copy in send_gx:
        copy.wait_recv()
    returned = dot(list_matrix(halo_rows[...], CAP), jnp.concatenate([in_gx[s] for s in range(S)], axis=0))
    local_back = jnp.concatenate([back_x[0:HALF, 0:C], back_x[0:HALF, C : 2 * C]], axis=0)
    input_grad[...] = hidden_grad[...] + local_back + returned

    sum_turn(4, (2,))
    sum_turn(5, (0, 1, 2))
    for copy in send_x + send_gh + send_h + send_gx + flying:
        copy.wait_send()


def finish(grad_scale, coarse_in, input_grad_in, summed, coarse, input_grad, conv_grad, down_grad):
    coarse[...] = coarse_in[...]
    input_grad[...] = input_grad_in[...]
    for k in range(K):
        part, at = (0, k) if k < 16 else (1, k - 16)
        conv_grad[k] = summed[part, at * C : (at + 1) * C, :].astype(F32) * grad_scale
    for o in range(O):
        for h in range(2):
            at = (2 * o + h) * C
            down_grad[o, :, h * C : (h + 1) * C] = summed[2, at : at + C, :].astype(F32) * grad_scale


def local(features, conv_weight, down_weight, neighbour_map, halo_rows, child_map, child_rows, out_grad):
    devices = lax.axis_size("shard")
    coarse, input_grad, summed = pl.pallas_call(
        kernel,
        out_shape=(
            jax.ShapeDtypeStruct((PD, C2), BF),
            jax.ShapeDtypeStruct((V, C), F32),
            jax.ShapeDtypeStruct((3, 2048, C), BF),
        ),
        scratch_shapes=[
            pltpu.VMEM((32, V), F32),
            pltpu.VMEM((K, V, 128), BF),
            pltpu.VMEM((O, PD), F32),
            pltpu.VMEM((O * PD, 128), BF),
            pltpu.VMEM((K, V, C), BF),
            pltpu.VMEM((PAIRS, 2 * C), BF),
            pltpu.VMEM((V, C), F32),
            pltpu.VMEM((V, C), BF),
            pltpu.VMEM((V, C), F32),
            pltpu.VMEM((V, C), BF),
            pltpu.VMEM((K, V, 2 * C), BF),
            pltpu.VMEM((PAIRS, 2 * C), F32),
            pltpu.VMEM((PAIRS, 2 * C), F32),
            pltpu.VMEM((S, CAP, C), BF),
            pltpu.VMEM((S, CAP, C), BF),
            pltpu.VMEM((S, CAP2, C), BF),
            pltpu.VMEM((S, CAP2, C), BF),
            pltpu.VMEM((S, CAP2, C), BF),
            pltpu.VMEM((S, CAP2, C), BF),
            pltpu.VMEM((S, CAP, C), BF),
            pltpu.VMEM((S, CAP, C), BF),
            pltpu.SemaphoreType.DMA((4, S)),
            pltpu.SemaphoreType.DMA((4, S)),
            pltpu.VMEM((3, 2, 1024, C), BF),
            pltpu.VMEM((3, 1024, C), BF),
            pltpu.VMEM((3, 16, 64, C), BF),
            pltpu.VMEM((3, 15, 64, C), BF),
            pltpu.VMEM((3, 4, 64, C), F32),
            pltpu.SemaphoreType.DMA((2, 3)),
            pltpu.SemaphoreType.DMA((2, 3)),
            pltpu.SemaphoreType.DMA((2, 3, 15)),
            pltpu.SemaphoreType.DMA((2, 3, 15)),
            pltpu.SemaphoreType.DMA((3, 3)),
            pltpu.SemaphoreType.DMA((3, 3)),
        ],
        compiler_params=pltpu.CompilerParams(
            collective_id=0, has_side_effects=True, vmem_limit_bytes=56 * 2**20
        ),
    )(features, conv_weight, down_weight, neighbour_map, halo_rows, child_map, child_rows, out_grad)
    grad_scale = 1.0 / math.sqrt(V * devices)
    return pl.pallas_call(
        lambda *refs: finish(grad_scale, *refs),
        out_shape=(
            jax.ShapeDtypeStruct((PD, C2), BF),
            jax.ShapeDtypeStruct((V, C), F32),
            jax.ShapeDtypeStruct((K, C, C), F32),
            jax.ShapeDtypeStruct((O, C, C2), F32),
        ),
        compiler_params=pltpu.CompilerParams(vmem_limit_bytes=60 * 2**20),
    )(coarse, input_grad, summed)


def solution(mesh):
    return jax.shard_map(
        local,
        mesh=mesh,
        in_specs=(
            P("shard", None),
            P(),
            P(),
            P(None, "shard"),
            P(None, "shard"),
            P(None, "shard"),
            P(None, "shard"),
            P("shard", None),
        ),
        out_specs=(P("shard", None), P("shard", None), P(), P()),
        check_vma=False,
    )
```

```python
import math

import jax
import jax.numpy as jnp
from jax import lax
from jax.experimental import pallas as pl
from jax.experimental.pallas import tpu as pltpu
from jax.sharding import PartitionSpec as P

MESH = pl.DeviceIdType.MESH
BF = jnp.bfloat16
F32 = jnp.float32
K = 27
O = 8
V = 1024
PD = 256
C = 128
C2 = 256
S = 4
CAP = 64
CAP2 = 32
HALF = V // 2
PAIRS = HALF + 128
OFFSETS = (-2, -1, 1, 2)
PLANES = ((2, 8, 32), (8, 32, 2), (32, 2, 8))
CHUNK = (64, 48, 64)
HOPS = [(i, j) for i in (2, 1, 3, 0) for j in (2, 1, 3, 0) if i or j]


def row_codes(rows, last, fold_received):
    received = rows >= V
    in_received = (rows >> 7) & 1 if fold_received else jnp.zeros_like(rows)
    side = jnp.where(received, in_received, (rows >> 9) & 1)
    block = jnp.where(received, 4, (rows >> 7) & 3)
    code = ((rows & 127) + 128) << block
    code = jnp.where(side == 1, -code, code)
    return jnp.where(rows >= last, 0, code).astype(F32)


def table_codes(shape, dim, start=0):
    place = lax.broadcasted_iota(jnp.int32, shape, dim) + start
    return (((place & 127) + 128) << (place >> 7)).astype(F32).astype(BF)


def pick_matrix(codes):
    size = jnp.abs(codes)
    names = table_codes((1, PAIRS), 1)
    one, zero = jnp.ones((), BF), jnp.zeros((), BF)
    return jnp.concatenate(
        [jnp.where(size == names[:, b * 128 : (b + 1) * 128], one, zero) for b in range(PAIRS // 128)], axis=1
    )


def spread_matrix(row, start, count):
    n = row.shape[1]
    size = jnp.broadcast_to(jnp.abs(row), (count, n)).astype(BF)
    names = table_codes((count, 128), 0, start)
    names = jnp.concatenate([names] * (n // 128), axis=1)
    return jnp.where(size == names, jnp.ones((), BF), jnp.zeros((), BF))


def pick_side(both, codes):
    both = both.astype(BF)
    return jnp.where(codes < 0, both[:, C:], both[:, :C])


def two_sides(rows, codes):
    zero = jnp.zeros((), BF)
    return jnp.concatenate([jnp.where(codes >= 0, rows, zero), jnp.where(codes < 0, rows, zero)], axis=1)


def dot(a, b):
    return jnp.dot(a, b, preferred_element_type=F32)


def dot_t(a, b):
    return lax.dot_general(a, b, (((1,), (1,)), ((), ())), preferred_element_type=F32)


def t_dot(a, b):
    return lax.dot_general(a, b, (((0,), (0,)), ((), ())), preferred_element_type=F32)


def unit_rows(rows, first, count):
    at = lax.broadcasted_iota(jnp.int32, (rows, 128 * count), 0)
    block = lax.broadcasted_iota(jnp.int32, (rows, 128 * count), 1) >> 7
    return (at == block + first).astype(F32).astype(BF)


def list_matrix(lists, cap):
    row = jnp.concatenate([lists[s : s + 1, :] for s in range(S)], axis=1)
    places = lax.broadcasted_iota(jnp.int32, (V, S * cap), 0)
    return (places == row).astype(F32).astype(BF)


def kernel(
    features_in, conv_weight_in, down_weight_in, neighbour_map_in, halo_rows_in, child_map_in, child_rows_in, out_grad_in,
    coarse, input_grad, summed,
    features, conv_weight, down_weight, neighbour_map, halo_rows, child_map, child_rows, out_grad, in_sems,
    codes_x, wide_x, wide_h, picked, table, pre, hidden, hidden_grad, pre_grad, z_all, back_x, spread_h,
    out_x, in_x, out_h, in_h, out_spread, in_spread, out_gx, in_gx, send_sem, recv_sem,
    terms, got_core, core_sum, got_plane, plane_sum,
    sum_send, sum_recv,
):
    n = lax.axis_size("shard")
    me = lax.axis_index("shard")
    core = lax.rem(me, 2)
    place = {stride: lax.rem(me // stride, 4) for stride in (2, 8, 32)}

    def shift(stride, by):
        return (lax.rem(place[stride] + by, 4) - place[stride]) * stride

    def device(by):
        return (lax.rem(me + by + n, n),)

    loads = [
        pltpu.make_async_copy(src, dst, in_sems.at[at])
        for at, (src, dst) in enumerate(
            (
                (halo_rows_in, halo_rows), (features_in, features), (neighbour_map_in, neighbour_map),
                (child_map_in, child_map), (out_grad_in, out_grad), (down_weight_in, down_weight),
                (conv_weight_in, conv_weight), (child_rows_in, child_rows),
            )
        )
    ]
    for load in loads:
        load.start()

    barrier = pltpu.get_barrier_semaphore()
    for by in OFFSETS:
        pl.semaphore_signal(barrier, inc=1, device_id=device(by), device_id_type=MESH)
    sibling = me + 1 - 2 * core
    pl.semaphore_signal(barrier, inc=1, device_id=(sibling,), device_id_type=MESH)
    for a, b, _ in PLANES:
        for i, j in HOPS:
            if i and j:
                to = me + shift(a, i) + shift(b, j)
                pl.semaphore_signal(barrier, inc=1, device_id=(to,), device_id_type=MESH)
        for i in (1, 2, 3):
            pl.semaphore_signal(barrier, inc=1, device_id=(me + shift(a, i),), device_id_type=MESH)

    def send(src, dst, sems, to):
        return pltpu.make_async_remote_copy(
            src_ref=src, dst_ref=dst, send_sem=sems[0], recv_sem=sems[1], device_id=(to,), device_id_type=MESH
        )

    flying = []

    def start_all(moves, whole, sems):
        for move in moves:
            move.start()
        group = send(whole, whole, sems, sibling)
        flying.append(group)
        return group

    def copies(which, src, dst, sign):
        sems = (send_sem.at[which], recv_sem.at[which])
        moves = [send(src.at[s], dst.at[s], sems, device(sign * OFFSETS[s])) for s in range(S)]
        return start_all(moves, src, sems)

    sums = [None] * 3

    def put_block(block, value):
        part = 0 if block < 16 else 1 if block < 28 else 2
        at = block - (0, 16, 28)[part]
        per_half = CHUNK[part] // 8
        terms[part, at // per_half, pl.ds(at % per_half * C, C), :] = value


    def sum_turn(turn, parts):
        for part in parts:
            if turn:
                sums[part].wait_recv()
            if turn < 5:
                sums[part] = sum_step(turn, part)

    def sum_step(turn, part):
        a, b, c = PLANES[part]
        size = CHUNK[part]
        here = place[a] * 4 + place[b]
        half = pl.ds(0, 16 * size)
        chunk = pl.ds(0, size)
        owned = pl.ds(pl.multiple_of(core * (16 * size) + here * size, 16), size)
        sems = (sum_send.at[turn, part], sum_recv.at[turn, part])
        fifteen = got_plane.at[part, :, chunk]
        if turn == 0:
            mine = terms.at[part, 1 - core, half]
            return start_all([send(mine, got_core.at[part, half], sems, sibling)], mine, sems)
        if turn == 1:
            total = (terms[part, core, half].astype(F32) + got_core[part, half].astype(F32)).astype(BF)
            for q in range(16):
                core_sum[part, q, chunk] = total[q * size : (q + 1) * size]
            moves = [
                send(
                    core_sum.at[part, lax.rem(place[a] + i, 4) * 4 + lax.rem(place[b] + j, 4), chunk],
                    got_plane.at[part, at, chunk], sems, me + shift(a, i) + shift(b, j),
                )
                for at, (i, j) in enumerate(HOPS)
            ]
            return start_all(moves, fifteen, sems)
        if turn == 2:
            total = core_sum[part, here, chunk].astype(F32)
            for at in range(15):
                total += got_plane[part, at, chunk].astype(F32)
            plane_sum[part, place[c], chunk] = total
            mine = plane_sum.at[part, place[c], chunk]
            moves = [send(mine, mine, sems, me + shift(c, i)) for i in (1, 2, 3)]
            return start_all(moves, plane_sum.at[part, pl.ds(0, 3), chunk], sems)
        if turn == 3:
            total = plane_sum[part, 0, chunk] + plane_sum[part, 1, chunk]
            total += plane_sum[part, 2, chunk] + plane_sum[part, 3, chunk]
            summed[part, owned] = total.astype(BF)
            mine = summed.at[part, owned]
            moves = [send(mine, mine, sems, me + shift(a, i) + shift(b, j)) for i, j in HOPS]
            return start_all(moves, fifteen, sems)
        mine = summed.at[part, pl.ds(pl.multiple_of(core * (16 * size), 16), 16 * size)]
        return start_all([send(mine, mine, sems, sibling)], mine, sems)

    loads[0].wait()
    loads[1].wait()
    chosen = t_dot(list_matrix(halo_rows[...], CAP), features[...]).astype(BF)
    for s in range(S):
        out_x[s] = chosen[s * CAP : (s + 1) * CAP]
    table[0:HALF, 0:C] = features[0:HALF, :]
    table[0:HALF, C : 2 * C] = features[HALF:V, :]

    loads[2].wait()
    codes_x[0:K, :] = row_codes(neighbour_map[...], V + S * CAP, True)
    codes_x[K:32, :] = jnp.zeros((32 - K, V), F32)
    turned_codes = codes_x[...].T.astype(BF)
    for k in range(0, K, 2):
        count = min(2, K - k)
        wide = dot(turned_codes, unit_rows(32, k, count)).astype(BF)
        for i in range(count):
            wide_x[k + i] = wide[:, i * 128 : (i + 1) * 128]
    pl.semaphore_wait(barrier, S + 37)
    send_x = copies(0, out_x, in_x, 1)

    for load in loads[3:]:
        load.wait()
    rows = child_map[...]
    plain = jnp.where(rows >= V + S * CAP2, 0, ((rows & 127) + 128) << (rows >> 7)).astype(F32)
    for o in range(O):
        total = dot(spread_matrix(plain[o : o + 1, :], 0, V + S * CAP2), out_grad[...]).astype(BF)
        spread_h[:, o * C2 : (o + 1) * C2] = total[0:V]
        for s in range(S):
            out_spread[s, :, o * C2 : (o + 1) * C2] = total[V + s * CAP2 : V + (s + 1) * CAP2]
    send_spread = copies(1, out_spread, in_spread, -1)
    total = jnp.zeros((V, C), F32)
    for o in range(O):
        total += dot_t(spread_h[:, o * C2 : (o + 1) * C2], down_weight[o])
    hidden_grad[...] = total
    send_x.wait_recv()
    for s in range(S):
        table[pl.ds(HALF + (s % 2) * CAP, CAP), pl.ds((s // 2) * C, C)] = in_x[s]
    pre[...] = jnp.zeros_like(pre)

    def forward(step, carry):
        k = step * 3
        group = []
        for i in range(3):
            codes = wide_x[k + i]
            rows = pick_side(dot(pick_matrix(codes), table[...]), codes)
            picked[k + i] = rows
            group.append(rows)
        weights = conv_weight[pl.ds(k, 3)].reshape(3 * C, C)
        pre[...] += dot(jnp.concatenate(group, axis=1), weights)
        return carry

    lax.fori_loop(0, K // 3, forward, 0)

    act = pre[...]
    gate = jax.nn.sigmoid(act)
    hidden[...] = (features[...].astype(F32) + act * gate).astype(BF)
    child_pick = list_matrix(child_rows[...], CAP2)
    chosen = t_dot(child_pick, hidden[...]).astype(BF)
    for s in range(S):
        out_h[s] = chosen[s * CAP2 : (s + 1) * CAP2]
    send_h = copies(2, out_h, in_h, 1)
    send_spread.wait_recv()
    turned_hidden = hidden[...].T
    turned_chosen = chosen.T
    for o in range(O):
        at = slice(o * C2, (o + 1) * C2)
        back_spread = jnp.concatenate([in_spread[s, :, at] for s in range(S)], axis=0)
        products = (dot(turned_hidden, spread_h[:, at]) + dot(turned_chosen, back_spread)).astype(BF)
        put_block(28 + 2 * o, products[:, 0:C])
        put_block(29 + 2 * o, products[:, C : 2 * C])
    sum_turn(0, (2,))

    returned = jnp.zeros((S * CAP2, C), F32)
    for o in range(O):
        back_spread = jnp.concatenate([in_spread[s, :, o * C2 : (o + 1) * C2] for s in range(S)], axis=0)
        returned += dot_t(back_spread, down_weight[o])
    grad_h = hidden_grad[...] + dot(child_pick, returned.astype(BF))
    hidden_grad[...] = grad_h
    pre_grad[...] = (grad_h * (gate * (1.0 + act * (1.0 - gate)))).astype(BF)

    turned_grad = pre_grad[...].T
    for k in range(0, K, 2):
        count = min(2, K - k)
        products = dot(turned_grad, jnp.concatenate([picked[k + i] for i in range(count)], axis=1))
        for i in range(count):
            put_block(k + i, products[:, i * C : (i + 1) * C].T.astype(BF))
        if k == 14:
            sum_turn(0, (0,))
    put_block(K, jnp.zeros((C, C), BF))
    sum_turn(0, (1,))
    sum_turn(1, (2,))
    sum_turn(1, (0,))

    back_x[...] = jnp.zeros_like(back_x)

    def backward(step, carry):
        k = step * 3
        z = dot_t(pre_grad[...], conv_weight[pl.ds(k, 3)].reshape(3 * C, C)).astype(BF)
        total = back_x[HALF:PAIRS, :]
        for i in range(3):
            z2 = two_sides(z[:, i * C : (i + 1) * C], wide_x[k + i])
            z_all[k + i] = z2
            total += dot(spread_matrix(codes_x[pl.ds(k + i, 1), :], HALF, 128), z2)
        back_x[HALF:PAIRS, :] = total
        return carry

    lax.fori_loop(0, 1, backward, 0)
    sum_turn(1, (1,))
    lax.fori_loop(1, 7, backward, 0)
    sum_turn(2, (2,))
    lax.fori_loop(7, 8, backward, 0)
    sum_turn(2, (0,))
    lax.fori_loop(8, K // 3, backward, 0)
    sum_turn(2, (1,))
    for s in range(S):
        out_gx[s] = back_x[pl.ds(HALF + (s % 2) * CAP, CAP), pl.ds((s // 2) * C, C)].astype(BF)
    send_gx = copies(3, out_gx, in_gx, -1)

    def backward_local(step, carry):
        k = step * 3
        total = back_x[0:HALF, :]
        for i in range(3):
            total += dot(spread_matrix(codes_x[pl.ds(k + i, 1), :], 0, HALF), z_all[k + i])
        back_x[0:HALF, :] = total
        return carry

    lax.fori_loop(0, 3, backward_local, 0)
    sum_turn(3, (2,))
    lax.fori_loop(3, 4, backward_local, 0)
    sum_turn(3, (0,))
    lax.fori_loop(4, 5, backward_local, 0)
    sum_turn(3, (1,))

    turned_codes = row_codes(child_map[...], V + S * CAP2, False).T.astype(BF)
    for o in range(0, O, 2):
        wide = dot(turned_codes, unit_rows(O, o, 2)).astype(BF)
        for i in range(2):
            wide_h[pl.ds((o + i) * PD, PD), :] = wide[:, i * 128 : (i + 1) * 128]
    table[0:HALF, 0:C] = hidden[0:HALF, :]
    table[0:HALF, C : 2 * C] = hidden[HALF:V, :]
    table[HALF:PAIRS, C : 2 * C] = jnp.zeros((128, C), BF)
    send_h.wait_recv()
    for s in range(S):
        table[pl.ds(HALF + s * CAP2, CAP2), 0:C] = in_h[s]
    total = jnp.zeros((PD, C2), F32)
    for o in range(O):
        codes = wide_h[pl.ds(o * PD, PD), :]
        rows = pick_side(dot(pick_matrix(codes), table[...]), codes)
        total += dot(rows, down_weight[o])
    coarse[...] = total.astype(BF)


    lax.fori_loop(5, K // 3, backward_local, 0)
    sum_turn(4, (2,))

    send_gx.wait_recv()
    returned = dot(list_matrix(halo_rows[...], CAP), jnp.concatenate([in_gx[s] for s in range(S)], axis=0))
    local_back = jnp.concatenate([back_x[0:HALF, 0:C], back_x[0:HALF, C : 2 * C]], axis=0)
    input_grad[...] = hidden_grad[...] + local_back + returned

    sum_turn(4, (0, 1))
    sum_turn(5, (0, 1, 2))
    for group in flying:
        group.wait_send()


FINISH = [(0, a, a + 4) for a in (0, 4, 8, 12)] + [(1, 0, 4), (1, 4, 8), (1, 8, 11)] + [(2, a, a + 4) for a in (0, 4, 8, 12)]


def finish(
    grad_scale, coarse_in, input_grad_in, summed_in, coarse, input_grad, conv_grad, down_grad,
    coarse_held, input_held, summed, conv_held, down_held, in_sems, out_sems,
):
    last = len(FINISH)
    loads = []
    for at, (part, first, end) in enumerate(FINISH):
        rows = pl.ds(first * C, (end - first) * C)
        loads.append(pltpu.make_async_copy(summed_in.at[part, rows], summed.at[part, rows], in_sems.at[at]))
    loads.append(pltpu.make_async_copy(coarse_in, coarse_held, in_sems.at[last]))
    loads.append(pltpu.make_async_copy(input_grad_in, input_held, in_sems.at[last + 1]))
    for load in loads:
        load.start()
    stores = []
    for at, (part, first, end) in enumerate(FINISH):
        loads[at].wait()
        for block in range(first, end):
            value = summed[part, block * C : (block + 1) * C, :].astype(F32) * grad_scale
            if part < 2:
                conv_held[part * 16 + block] = value
            else:
                down_held[block // 2, :, block % 2 * C : (block % 2 + 1) * C] = value
        if part < 2:
            held, out, rows = conv_held, conv_grad, pl.ds(part * 16 + first, end - first)
        else:
            held, out, rows = down_held, down_grad, pl.ds(first // 2, (end - first) // 2)
        stores.append(pltpu.make_async_copy(held.at[rows], out.at[rows], out_sems.at[at]))
        stores[-1].start()
    for at, (held, out) in enumerate(((coarse_held, coarse), (input_held, input_grad))):
        loads[last + at].wait()
        stores.append(pltpu.make_async_copy(held, out, out_sems.at[last + at]))
        stores[-1].start()
    for store in stores:
        store.wait()


def local(features, conv_weight, down_weight, neighbour_map, halo_rows, child_map, child_rows, out_grad):
    devices = lax.axis_size("shard")
    inputs = (features, conv_weight, down_weight, neighbour_map, halo_rows, child_map, child_rows, out_grad)
    coarse, input_grad, summed = pl.pallas_call(
        kernel,
        out_shape=(
            jax.ShapeDtypeStruct((PD, C2), BF),
            jax.ShapeDtypeStruct((V, C), F32),
            jax.ShapeDtypeStruct((3, 2048, C), BF),
        ),
        in_specs=[pl.BlockSpec(memory_space=pl.ANY)] * 8,
        scratch_shapes=[pltpu.VMEM(value.shape, value.dtype) for value in inputs] + [
            pltpu.SemaphoreType.DMA((8,)),
            pltpu.VMEM((32, V), F32),
            pltpu.VMEM((K, V, 128), BF),
            pltpu.VMEM((O * PD, 128), BF),
            pltpu.VMEM((K, V, C), BF),
            pltpu.VMEM((PAIRS, 2 * C), BF),
            pltpu.VMEM((V, C), F32),
            pltpu.VMEM((V, C), BF),
            pltpu.VMEM((V, C), F32),
            pltpu.VMEM((V, C), BF),
            pltpu.VMEM((K, V, 2 * C), BF),
            pltpu.VMEM((PAIRS, 2 * C), F32),
            pltpu.VMEM((V, O * C2), BF),
            pltpu.VMEM((S, CAP, C), BF),
            pltpu.VMEM((S, CAP, C), BF),
            pltpu.VMEM((S, CAP2, C), BF),
            pltpu.VMEM((S, CAP2, C), BF),
            pltpu.VMEM((S, CAP2, O * C2), BF),
            pltpu.VMEM((S, CAP2, O * C2), BF),
            pltpu.VMEM((S, CAP, C), BF),
            pltpu.VMEM((S, CAP, C), BF),
            pltpu.SemaphoreType.DMA((4,)),
            pltpu.SemaphoreType.DMA((4,)),
            pltpu.VMEM((3, 2, 1024, C), BF),
            pltpu.VMEM((3, 1024, C), BF),
            pltpu.VMEM((3, 16, 64, C), BF),
            pltpu.VMEM((3, 15, 64, C), BF),
            pltpu.VMEM((3, 4, 64, C), F32),
            pltpu.SemaphoreType.DMA((5, 3)),
            pltpu.SemaphoreType.DMA((5, 3)),
        ],
        compiler_params=pltpu.CompilerParams(
            collective_id=0, has_side_effects=True, vmem_limit_bytes=60 * 2**20
        ),
    )(*inputs)
    grad_scale = 1.0 / math.sqrt(V * devices)
    return pl.pallas_call(
        lambda *refs: finish(grad_scale, *refs),
        out_shape=(
            jax.ShapeDtypeStruct((PD, C2), BF),
            jax.ShapeDtypeStruct((V, C), F32),
            jax.ShapeDtypeStruct((K, C, C), F32),
            jax.ShapeDtypeStruct((O, C, C2), F32),
        ),
        in_specs=[pl.BlockSpec(memory_space=pl.ANY)] * 3,
        out_specs=[pl.BlockSpec(memory_space=pl.ANY)] * 4,
        scratch_shapes=[
            pltpu.VMEM((PD, C2), BF),
            pltpu.VMEM((V, C), F32),
            pltpu.VMEM((3, 2048, C), BF),
            pltpu.VMEM((K, C, C), F32),
            pltpu.VMEM((O, C, C2), F32),
            pltpu.SemaphoreType.DMA((len(FINISH) + 2,)),
            pltpu.SemaphoreType.DMA((len(FINISH) + 2,)),
        ],
        compiler_params=pltpu.CompilerParams(vmem_limit_bytes=60 * 2**20),
    )(coarse, input_grad, summed)


def solution(mesh):
    return jax.shard_map(
        local,
        mesh=mesh,
        in_specs=(
            P("shard", None),
            P(),
            P(),
            P(None, "shard"),
            P(None, "shard"),
            P(None, "shard"),
            P(None, "shard"),
            P("shard", None),
        ),
        out_specs=(P("shard", None), P("shard", None), P(), P()),
        check_vma=False,
    )
```

```python
import math

import jax
import jax.numpy as jnp
from jax import lax
from jax.experimental import pallas as pl
from jax.experimental.pallas import tpu as pltpu
from jax.sharding import PartitionSpec as P

MESH = pl.DeviceIdType.MESH
BF = jnp.bfloat16
F32 = jnp.float32
K = 27
O = 8
V = 1024
PD = 256
C = 128
C2 = 256
S = 4
CAP = 64
CAP2 = 32
HALF = V // 2
PAIRS = HALF + 128
OFFSETS = (-2, -1, 1, 2)
EARLY = 2
PLANES = ((2, 8, 32), (8, 32, 2), (32, 2, 8))
CHUNK = (64, 48, 64)
HOPS = [(i, j) for i in (2, 1, 3, 0) for j in (2, 1, 3, 0) if i or j]


def row_codes(rows, last, fold_received):
    received = rows >= V
    in_received = (rows >> 7) & 1 if fold_received else jnp.zeros_like(rows)
    side = jnp.where(received, in_received, (rows >> 9) & 1)
    block = jnp.where(received, 4, (rows >> 7) & 3)
    code = ((rows & 127) + 128) << block
    code = jnp.where(side == 1, -code, code)
    return jnp.where(rows >= last, 0, code).astype(F32)


def table_codes(shape, dim, start=0):
    place = lax.broadcasted_iota(jnp.int32, shape, dim) + start
    return (((place & 127) + 128) << (place >> 7)).astype(F32).astype(BF)


def pick_matrix(codes, first=0, end=PAIRS // 128):
    size = jnp.abs(codes)
    names = table_codes((1, PAIRS), 1)
    one, zero = jnp.ones((), BF), jnp.zeros((), BF)
    return jnp.concatenate(
        [jnp.where(size == names[:, b * 128 : (b + 1) * 128], one, zero) for b in range(first, end)], axis=1
    )


def spread_matrix(row, start, count):
    n = row.shape[1]
    size = jnp.broadcast_to(jnp.abs(row), (count, n)).astype(BF)
    names = table_codes((count, 128), 0, start)
    names = jnp.concatenate([names] * (n // 128), axis=1)
    return jnp.where(size == names, jnp.ones((), BF), jnp.zeros((), BF))


def pick_side(both, codes):
    both = both.astype(BF)
    return jnp.where(codes < 0, both[:, C:], both[:, :C])


def two_sides(rows, codes):
    zero = jnp.zeros((), BF)
    return jnp.concatenate([jnp.where(codes >= 0, rows, zero), jnp.where(codes < 0, rows, zero)], axis=1)


def dot(a, b):
    return jnp.dot(a, b, preferred_element_type=F32)


def dot_t(a, b):
    return lax.dot_general(a, b, (((1,), (1,)), ((), ())), preferred_element_type=F32)


def t_dot(a, b):
    return lax.dot_general(a, b, (((0,), (0,)), ((), ())), preferred_element_type=F32)


def unit_rows(rows, first, count):
    at = lax.broadcasted_iota(jnp.int32, (rows, 128 * count), 0)
    block = lax.broadcasted_iota(jnp.int32, (rows, 128 * count), 1) >> 7
    return (at == block + first).astype(F32).astype(BF)


def list_matrix(lists, cap):
    row = jnp.concatenate([lists[s : s + 1, :] for s in range(S)], axis=1)
    places = lax.broadcasted_iota(jnp.int32, (V, S * cap), 0)
    return (places == row).astype(F32).astype(BF)


def kernel(
    features_in, conv_weight_in, down_weight_in, neighbour_map_in, halo_rows_in, child_map_in, child_rows_in, out_grad_in,
    coarse_out, input_grad_out, summed_out,
    coarse, input_grad, summed, out_sems,
    features, conv_weight, down_weight, neighbour_map, halo_rows, child_map, child_rows, out_grad, in_sems,
    codes_x, wide_x, wide_h, picked, table, pre, hidden, hidden_grad, pre_grad, z_all, back_x, spread_h,
    out_x, in_x, out_h, in_h, out_spread, in_spread, out_gx, in_gx, send_sem, recv_sem,
    terms, got_core, core_sum, got_plane, plane_sum,
    sum_send, sum_recv,
):
    n = lax.axis_size("shard")
    me = lax.axis_index("shard")
    core = lax.rem(me, 2)
    place = {stride: lax.rem(me // stride, 4) for stride in (2, 8, 32)}

    def shift(stride, by):
        return (lax.rem(place[stride] + by, 4) - place[stride]) * stride

    def device(by):
        return (lax.rem(me + by + n, n),)

    loads = [
        pltpu.make_async_copy(src, dst, in_sems.at[at])
        for at, (src, dst) in enumerate(
            (
                (halo_rows_in, halo_rows), (features_in, features), (neighbour_map_in, neighbour_map),
                (child_map_in, child_map), (out_grad_in, out_grad), (down_weight_in, down_weight),
                (conv_weight_in, conv_weight), (child_rows_in, child_rows),
            )
        )
    ]
    for load in loads:
        load.start()

    results = [
        pltpu.make_async_copy(coarse, coarse_out, out_sems.at[0]),
        pltpu.make_async_copy(input_grad, input_grad_out, out_sems.at[1]),
    ] + [pltpu.make_async_copy(summed.at[part], summed_out.at[part], out_sems.at[2 + part]) for part in range(3)]

    barrier = pltpu.get_barrier_semaphore()
    for by in OFFSETS:
        pl.semaphore_signal(barrier, inc=1, device_id=device(by), device_id_type=MESH)
    sibling = me + 1 - 2 * core
    pl.semaphore_signal(barrier, inc=1, device_id=(sibling,), device_id_type=MESH)
    for a, b, _ in PLANES:
        for i, j in HOPS:
            if i and j:
                to = me + shift(a, i) + shift(b, j)
                pl.semaphore_signal(barrier, inc=1, device_id=(to,), device_id_type=MESH)
        for i in (1, 2, 3):
            pl.semaphore_signal(barrier, inc=1, device_id=(me + shift(a, i),), device_id_type=MESH)

    def send(src, dst, sems, to):
        return pltpu.make_async_remote_copy(
            src_ref=src, dst_ref=dst, send_sem=sems[0], recv_sem=sems[1], device_id=(to,), device_id_type=MESH
        )

    flying = []

    def start_all(moves, whole, sems):
        for move in moves:
            move.start()
        group = send(whole, whole, sems, sibling)
        flying.append(group)
        return group

    def copies(which, src, dst, sign):
        sems = (send_sem.at[which], recv_sem.at[which])
        moves = [send(src.at[s], dst.at[s], sems, device(sign * OFFSETS[s])) for s in range(S)]
        return start_all(moves, src, sems)

    sums = [None] * 3

    def put_block(block, value):
        part = 0 if block < 16 else 1 if block < 28 else 2
        at = block - (0, 16, 28)[part]
        per_half = CHUNK[part] // 8
        terms[part, at // per_half, pl.ds(at % per_half * C, C), :] = value


    def sum_turn(turn, parts):
        for part in parts:
            if turn:
                sums[part].wait_recv()
            if turn < 5:
                sums[part] = sum_step(turn, part)

    def sum_step(turn, part):
        a, b, c = PLANES[part]
        size = CHUNK[part]
        here = place[a] * 4 + place[b]
        half = pl.ds(0, 16 * size)
        chunk = pl.ds(0, size)
        owned = pl.ds(pl.multiple_of(core * (16 * size) + here * size, 16), size)
        sems = (sum_send.at[turn, part], sum_recv.at[turn, part])
        fifteen = got_plane.at[part, :, chunk]
        if turn == 0:
            mine = terms.at[part, 1 - core, half]
            return start_all([send(mine, got_core.at[part, half], sems, sibling)], mine, sems)
        if turn == 1:
            total = (terms[part, core, half].astype(F32) + got_core[part, half].astype(F32)).astype(BF)
            for q in range(16):
                core_sum[part, q, chunk] = total[q * size : (q + 1) * size]
            moves = [
                send(
                    core_sum.at[part, lax.rem(place[a] + i, 4) * 4 + lax.rem(place[b] + j, 4), chunk],
                    got_plane.at[part, at, chunk], sems, me + shift(a, i) + shift(b, j),
                )
                for at, (i, j) in enumerate(HOPS)
            ]
            return start_all(moves, fifteen, sems)
        if turn == 2:
            total = core_sum[part, here, chunk].astype(F32)
            for at in range(15):
                total += got_plane[part, at, chunk].astype(F32)
            plane_sum[part, place[c], chunk] = total
            mine = plane_sum.at[part, place[c], chunk]
            moves = [send(mine, mine, sems, me + shift(c, i)) for i in (1, 2, 3)]
            return start_all(moves, plane_sum.at[part, pl.ds(0, 3), chunk], sems)
        if turn == 3:
            total = plane_sum[part, 0, chunk] + plane_sum[part, 1, chunk]
            total += plane_sum[part, 2, chunk] + plane_sum[part, 3, chunk]
            summed[part, owned] = total.astype(BF)
            mine = summed.at[part, owned]
            moves = [send(mine, mine, sems, me + shift(a, i) + shift(b, j)) for i, j in HOPS]
            return start_all(moves, fifteen, sems)
        mine = summed.at[part, pl.ds(pl.multiple_of(core * (16 * size), 16), 16 * size)]
        return start_all([send(mine, mine, sems, sibling)], mine, sems)

    loads[0].wait()
    loads[1].wait()
    chosen = t_dot(list_matrix(halo_rows[...], CAP), features[...]).astype(BF)
    for s in range(S):
        out_x[s] = chosen[s * CAP : (s + 1) * CAP]
    table[0:HALF, 0:C] = features[0:HALF, :]
    table[0:HALF, C : 2 * C] = features[HALF:V, :]

    loads[2].wait()
    codes_x[0:K, :] = row_codes(neighbour_map[...], V + S * CAP, True)
    codes_x[K:32, :] = jnp.zeros((32 - K, V), F32)
    turned_codes = codes_x[...].T.astype(BF)
    for k in range(0, K, 2):
        count = min(2, K - k)
        wide = dot(turned_codes, unit_rows(32, k, count)).astype(BF)
        for i in range(count):
            wide_x[k + i] = wide[:, i * 128 : (i + 1) * 128]
    pl.semaphore_wait(barrier, S + 37)
    send_x = copies(0, out_x, in_x, 1)

    for load in loads[3:]:
        load.wait()
    rows = child_map[...]
    plain = jnp.where(rows >= V + S * CAP2, 0, ((rows & 127) + 128) << (rows >> 7)).astype(F32)
    for o in range(O):
        total = dot(spread_matrix(plain[o : o + 1, :], 0, V + S * CAP2), out_grad[...]).astype(BF)
        spread_h[:, o * C2 : (o + 1) * C2] = total[0:V]
        for s in range(S):
            out_spread[s, :, o * C2 : (o + 1) * C2] = total[V + s * CAP2 : V + (s + 1) * CAP2]
    send_spread = copies(1, out_spread, in_spread, -1)
    total = jnp.zeros((V, C), F32)
    for o in range(O):
        total += dot_t(spread_h[:, o * C2 : (o + 1) * C2], down_weight[o])
    hidden_grad[...] = total
    def pick_local(step, carry):
        for i in range(3):
            k = step * 3 + i
            z_all[k] = dot(pick_matrix(wide_x[k], 0, 4), table[0:HALF, :]).astype(BF)
        return carry

    lax.fori_loop(0, EARLY, pick_local, 0)
    send_x.wait_recv()
    for s in range(S):
        table[pl.ds(HALF + (s % 2) * CAP, CAP), pl.ds((s // 2) * C, C)] = in_x[s]
    pre[...] = jnp.zeros_like(pre)

    def multiply(k, group):
        weights = conv_weight[pl.ds(k, len(group))].reshape(len(group) * C, C)
        pre[...] += dot(jnp.concatenate(group, axis=1), weights)

    def forward_early(step, carry):
        group = []
        for i in range(3):
            k = step * 3 + i
            codes = wide_x[k]
            both = dot(pick_matrix(codes, 4, 5), table[HALF:PAIRS, :]).astype(BF) + z_all[k]
            rows = jnp.where(codes < 0, both[:, C:], both[:, :C])
            picked[k] = rows
            group.append(rows)
        multiply(step * 3, group)
        return carry

    lax.fori_loop(0, EARLY, forward_early, 0)

    def forward(step, carry):
        group = []
        for i in range(3):
            k = step * 3 + i
            codes = wide_x[k]
            rows = pick_side(dot(pick_matrix(codes), table[...]), codes)
            picked[k] = rows
            group.append(rows)
        multiply(step * 3, group)
        return carry

    lax.fori_loop(EARLY, K // 3, forward, 0)

    act = pre[...]
    gate = jax.nn.sigmoid(act)
    hidden[...] = (features[...].astype(F32) + act * gate).astype(BF)
    child_pick = list_matrix(child_rows[...], CAP2)
    chosen = t_dot(child_pick, hidden[...]).astype(BF)
    for s in range(S):
        out_h[s] = chosen[s * CAP2 : (s + 1) * CAP2]
    send_h = copies(2, out_h, in_h, 1)
    send_spread.wait_recv()
    turned_hidden = hidden[...].T
    turned_chosen = chosen.T
    for o in range(O):
        at = slice(o * C2, (o + 1) * C2)
        back_spread = jnp.concatenate([in_spread[s, :, at] for s in range(S)], axis=0)
        products = (dot(turned_hidden, spread_h[:, at]) + dot(turned_chosen, back_spread)).astype(BF)
        put_block(28 + 2 * o, products[:, 0:C])
        put_block(29 + 2 * o, products[:, C : 2 * C])
    sum_turn(0, (2,))

    returned = jnp.zeros((S * CAP2, C), F32)
    for o in range(O):
        back_spread = jnp.concatenate([in_spread[s, :, o * C2 : (o + 1) * C2] for s in range(S)], axis=0)
        returned += dot_t(back_spread, down_weight[o])
    grad_h = hidden_grad[...] + dot(child_pick, returned.astype(BF))
    hidden_grad[...] = grad_h
    pre_grad[...] = (grad_h * (gate * (1.0 + act * (1.0 - gate)))).astype(BF)

    turned_grad = pre_grad[...].T
    for k in range(0, K, 2):
        count = min(2, K - k)
        products = dot(turned_grad, jnp.concatenate([picked[k + i] for i in range(count)], axis=1))
        for i in range(count):
            put_block(k + i, products[:, i * C : (i + 1) * C].T.astype(BF))
        if k == 14:
            sum_turn(0, (0,))
            sum_turn(1, (2,))
    put_block(K, jnp.zeros((C, C), BF))
    sum_turn(0, (1,))
    sum_turn(1, (0,))

    back_x[...] = jnp.zeros_like(back_x)

    def backward(step, carry):
        k = step * 3
        z = dot_t(pre_grad[...], conv_weight[pl.ds(k, 3)].reshape(3 * C, C)).astype(BF)
        total = back_x[HALF:PAIRS, :]
        for i in range(3):
            z2 = two_sides(z[:, i * C : (i + 1) * C], wide_x[k + i])
            z_all[k + i] = z2
            total += dot(spread_matrix(codes_x[pl.ds(k + i, 1), :], HALF, 128), z2)
        back_x[HALF:PAIRS, :] = total
        return carry

    lax.fori_loop(0, 1, backward, 0)
    sum_turn(1, (1,))
    lax.fori_loop(1, K // 3, backward, 0)
    for s in range(S):
        out_gx[s] = back_x[pl.ds(HALF + (s % 2) * CAP, CAP), pl.ds((s // 2) * C, C)].astype(BF)
    send_gx = copies(3, out_gx, in_gx, -1)

    def backward_local(step, carry):
        k = step * 3
        total = back_x[0:HALF, :]
        for i in range(3):
            total += dot(spread_matrix(codes_x[pl.ds(k + i, 1), :], 0, HALF), z_all[k + i])
        back_x[0:HALF, :] = total
        return carry

    sum_turn(2, (2, 0, 1))
    lax.fori_loop(0, 4, backward_local, 0)
    sum_turn(3, (2, 0, 1))

    turned_codes = row_codes(child_map[...], V + S * CAP2, False).T.astype(BF)
    for o in range(0, O, 2):
        wide = dot(turned_codes, unit_rows(O, o, 2)).astype(BF)
        for i in range(2):
            wide_h[pl.ds((o + i) * PD, PD), :] = wide[:, i * 128 : (i + 1) * 128]
    table[0:HALF, 0:C] = hidden[0:HALF, :]
    table[0:HALF, C : 2 * C] = hidden[HALF:V, :]
    table[HALF:PAIRS, C : 2 * C] = jnp.zeros((128, C), BF)
    send_h.wait_recv()
    for s in range(S):
        table[pl.ds(HALF + s * CAP2, CAP2), 0:C] = in_h[s]
    total = jnp.zeros((PD, C2), F32)
    for o in range(O):
        codes = wide_h[pl.ds(o * PD, PD), :]
        rows = pick_side(dot(pick_matrix(codes), table[...]), codes)
        total += dot(rows, down_weight[o])
    coarse[...] = total.astype(BF)
    results[0].start()


    lax.fori_loop(4, K // 3, backward_local, 0)

    send_gx.wait_recv()
    returned = dot(list_matrix(halo_rows[...], CAP), jnp.concatenate([in_gx[s] for s in range(S)], axis=0))
    local_back = jnp.concatenate([back_x[0:HALF, 0:C], back_x[0:HALF, C : 2 * C]], axis=0)
    input_grad[...] = hidden_grad[...] + local_back + returned

    results[1].start()
    sum_turn(4, (2, 0, 1))
    for part in (2, 0, 1):
        sum_turn(5, (part,))
        results[2 + part].start()
    for result in results:
        result.wait()
    for group in flying:
        group.wait_send()


FINISH = [(0, a, a + 4) for a in (0, 4, 8, 12)] + [(1, 0, 4), (1, 4, 8), (1, 8, 11)] + [(2, a, a + 4) for a in (0, 4, 8, 12)]


def finish(
    grad_scale, coarse_in, input_grad_in, summed_in, coarse, input_grad, conv_grad, down_grad,
    coarse_held, input_held, summed, conv_held, down_held, in_sems, out_sems,
):
    last = len(FINISH)
    loads = []
    for at, (part, first, end) in enumerate(FINISH):
        rows = pl.ds(first * C, (end - first) * C)
        loads.append(pltpu.make_async_copy(summed_in.at[part, rows], summed.at[part, rows], in_sems.at[at]))
    loads.append(pltpu.make_async_copy(coarse_in, coarse_held, in_sems.at[last]))
    loads.append(pltpu.make_async_copy(input_grad_in, input_held, in_sems.at[last + 1]))
    for load in loads:
        load.start()
    stores = []
    for at, (part, first, end) in enumerate(FINISH):
        loads[at].wait()
        for block in range(first, end):
            value = summed[part, block * C : (block + 1) * C, :].astype(F32) * grad_scale
            if part < 2:
                conv_held[part * 16 + block] = value
            else:
                down_held[block // 2, :, block % 2 * C : (block % 2 + 1) * C] = value
        if part < 2:
            held, out, rows = conv_held, conv_grad, pl.ds(part * 16 + first, end - first)
        else:
            held, out, rows = down_held, down_grad, pl.ds(first // 2, (end - first) // 2)
        stores.append(pltpu.make_async_copy(held.at[rows], out.at[rows], out_sems.at[at]))
        stores[-1].start()
    for at, (held, out) in enumerate(((coarse_held, coarse), (input_held, input_grad))):
        loads[last + at].wait()
        stores.append(pltpu.make_async_copy(held, out, out_sems.at[last + at]))
        stores[-1].start()
    for store in stores:
        store.wait()


def local(features, conv_weight, down_weight, neighbour_map, halo_rows, child_map, child_rows, out_grad):
    devices = lax.axis_size("shard")
    inputs = (features, conv_weight, down_weight, neighbour_map, halo_rows, child_map, child_rows, out_grad)
    coarse, input_grad, summed = pl.pallas_call(
        kernel,
        out_shape=(
            jax.ShapeDtypeStruct((PD, C2), BF),
            jax.ShapeDtypeStruct((V, C), F32),
            jax.ShapeDtypeStruct((3, 2048, C), BF),
        ),
        in_specs=[pl.BlockSpec(memory_space=pl.ANY)] * 8,
        out_specs=[pl.BlockSpec(memory_space=pl.ANY)] * 3,
        scratch_shapes=[
            pltpu.VMEM((PD, C2), BF),
            pltpu.VMEM((V, C), F32),
            pltpu.VMEM((3, 2048, C), BF),
            pltpu.SemaphoreType.DMA((5,)),
        ] + [pltpu.VMEM(value.shape, value.dtype) for value in inputs] + [
            pltpu.SemaphoreType.DMA((8,)),
            pltpu.VMEM((32, V), F32),
            pltpu.VMEM((K, V, 128), BF),
            pltpu.VMEM((O * PD, 128), BF),
            pltpu.VMEM((K, V, C), BF),
            pltpu.VMEM((PAIRS, 2 * C), BF),
            pltpu.VMEM((V, C), F32),
            pltpu.VMEM((V, C), BF),
            pltpu.VMEM((V, C), F32),
            pltpu.VMEM((V, C), BF),
            pltpu.VMEM((K, V, 2 * C), BF),
            pltpu.VMEM((PAIRS, 2 * C), F32),
            pltpu.VMEM((V, O * C2), BF),
            pltpu.VMEM((S, CAP, C), BF),
            pltpu.VMEM((S, CAP, C), BF),
            pltpu.VMEM((S, CAP2, C), BF),
            pltpu.VMEM((S, CAP2, C), BF),
            pltpu.VMEM((S, CAP2, O * C2), BF),
            pltpu.VMEM((S, CAP2, O * C2), BF),
            pltpu.VMEM((S, CAP, C), BF),
            pltpu.VMEM((S, CAP, C), BF),
            pltpu.SemaphoreType.DMA((4,)),
            pltpu.SemaphoreType.DMA((4,)),
            pltpu.VMEM((3, 2, 1024, C), BF),
            pltpu.VMEM((3, 1024, C), BF),
            pltpu.VMEM((3, 16, 64, C), BF),
            pltpu.VMEM((3, 15, 64, C), BF),
            pltpu.VMEM((3, 4, 64, C), F32),
            pltpu.SemaphoreType.DMA((5, 3)),
            pltpu.SemaphoreType.DMA((5, 3)),
        ],
        compiler_params=pltpu.CompilerParams(
            collective_id=0, has_side_effects=True, vmem_limit_bytes=60 * 2**20
        ),
    )(*inputs)
    grad_scale = 1.0 / math.sqrt(V * devices)
    return pl.pallas_call(
        lambda *refs: finish(grad_scale, *refs),
        out_shape=(
            jax.ShapeDtypeStruct((PD, C2), BF),
            jax.ShapeDtypeStruct((V, C), F32),
            jax.ShapeDtypeStruct((K, C, C), F32),
            jax.ShapeDtypeStruct((O, C, C2), F32),
        ),
        in_specs=[pl.BlockSpec(memory_space=pl.ANY)] * 3,
        out_specs=[pl.BlockSpec(memory_space=pl.ANY)] * 4,
        scratch_shapes=[
            pltpu.VMEM((PD, C2), BF),
            pltpu.VMEM((V, C), F32),
            pltpu.VMEM((3, 2048, C), BF),
            pltpu.VMEM((K, C, C), F32),
            pltpu.VMEM((O, C, C2), F32),
            pltpu.SemaphoreType.DMA((len(FINISH) + 2,)),
            pltpu.SemaphoreType.DMA((len(FINISH) + 2,)),
        ],
        compiler_params=pltpu.CompilerParams(vmem_limit_bytes=60 * 2**20),
    )(coarse, input_grad, summed)


def solution(mesh):
    return jax.shard_map(
        local,
        mesh=mesh,
        in_specs=(
            P("shard", None),
            P(),
            P(),
            P(None, "shard"),
            P(None, "shard"),
            P(None, "shard"),
            P(None, "shard"),
            P("shard", None),
        ),
        out_specs=(P("shard", None), P("shard", None), P(), P()),
        check_vma=False,
    )
```

```python
import math

import jax
import jax.numpy as jnp
from jax import lax
from jax.experimental import pallas as pl
from jax.experimental.pallas import tpu as pltpu
from jax.sharding import PartitionSpec as P

MESH = pl.DeviceIdType.MESH
BF = jnp.bfloat16
F32 = jnp.float32
K = 27
SELF = 13
G = K - 1
O = 8
V = 1024
PD = 256
C = 128
C2 = 256
S = 4
CAP = 64
CAP2 = 32
HALF = V // 2
PAIRS = HALF + 128
OFFSETS = (-2, -1, 1, 2)
LOCAL_FIRST = 3
EARLY = 2
PLANES = ((2, 8, 32), (8, 32, 2), (32, 2, 8))
CHUNK = (64, 48, 64)
HOPS = [(i, j) for i in (2, 1, 3, 0) for j in (2, 1, 3, 0) if i or j]


def row_codes(rows, last, fold_received):
    received = rows >= V
    in_received = (rows >> 7) & 1 if fold_received else jnp.zeros_like(rows)
    side = jnp.where(received, in_received, (rows >> 9) & 1)
    block = jnp.where(received, 4, (rows >> 7) & 3)
    code = ((rows & 127) + 128) << block
    code = jnp.where(side == 1, -code, code)
    return jnp.where(rows >= last, 0, code).astype(F32)


def table_codes(shape, dim, start=0):
    place = lax.broadcasted_iota(jnp.int32, shape, dim) + start
    return (((place & 127) + 128) << (place >> 7)).astype(F32).astype(BF)


def pick_matrix(codes, first=0, end=PAIRS // 128):
    size = jnp.abs(codes)
    names = table_codes((1, PAIRS), 1)
    one, zero = jnp.ones((), BF), jnp.zeros((), BF)
    return jnp.concatenate(
        [jnp.where(size == names[:, b * 128 : (b + 1) * 128], one, zero) for b in range(first, end)], axis=1
    )


def spread_matrix(row, start, count):
    n = row.shape[1]
    size = jnp.broadcast_to(jnp.abs(row), (count, n)).astype(BF)
    names = table_codes((count, 128), 0, start)
    names = jnp.concatenate([names] * (n // 128), axis=1)
    return jnp.where(size == names, jnp.ones((), BF), jnp.zeros((), BF))


def pick_side(both, codes):
    both = both.astype(BF)
    return jnp.where(codes < 0, both[:, C:], both[:, :C])


def two_sides(rows, codes):
    zero = jnp.zeros((), BF)
    return jnp.concatenate([jnp.where(codes >= 0, rows, zero), jnp.where(codes < 0, rows, zero)], axis=1)


def dot(a, b):
    return jnp.dot(a, b, preferred_element_type=F32)


def dot_t(a, b):
    return lax.dot_general(a, b, (((1,), (1,)), ((), ())), preferred_element_type=F32)


def t_dot(a, b):
    return lax.dot_general(a, b, (((0,), (0,)), ((), ())), preferred_element_type=F32)


def unit_rows(rows, first, count):
    at = lax.broadcasted_iota(jnp.int32, (rows, 128 * count), 0)
    block = lax.broadcasted_iota(jnp.int32, (rows, 128 * count), 1) >> 7
    return (at == block + first).astype(F32).astype(BF)


def list_matrix(lists, cap):
    row = jnp.concatenate([lists[s : s + 1, :] for s in range(S)], axis=1)
    places = lax.broadcasted_iota(jnp.int32, (V, S * cap), 0)
    return (places == row).astype(F32).astype(BF)


def kernel(
    features_in, conv_weight_in, down_weight_in, neighbour_map_in, halo_rows_in, child_map_in, child_rows_in, out_grad_in,
    coarse, input_grad, summed,
    features, conv_weight, down_weight, neighbour_map, halo_rows, child_map, child_rows, out_grad, in_sems,
    codes_x, wide_x, wide_h, picked, table, pre, hidden, hidden_grad, pre_grad, z_all, back_x, spread_h,
    out_x, in_x, out_h, in_h, out_spread, in_spread, out_gx, in_gx, send_sem, recv_sem,
    terms, got_core, core_sum, got_plane, plane_sum,
    sum_send, sum_recv,
):
    n = lax.axis_size("shard")
    me = lax.axis_index("shard")
    core = lax.rem(me, 2)
    place = {stride: lax.rem(me // stride, 4) for stride in (2, 8, 32)}

    def shift(stride, by):
        return (lax.rem(place[stride] + by, 4) - place[stride]) * stride

    def device(by):
        return (lax.rem(me + by + n, n),)

    loads = [
        pltpu.make_async_copy(src, dst, in_sems.at[at])
        for at, (src, dst) in enumerate(
            (
                (halo_rows_in, halo_rows), (features_in, features), (neighbour_map_in, neighbour_map),
                (child_map_in, child_map), (out_grad_in, out_grad), (down_weight_in, down_weight),
                (child_rows_in, child_rows),
                (conv_weight_in.at[pl.ds(0, SELF)], conv_weight.at[pl.ds(0, SELF)]),
                (conv_weight_in.at[pl.ds(SELF + 1, G - SELF - 1)], conv_weight.at[pl.ds(SELF + 1, G - SELF - 1)]),
                (conv_weight_in.at[G], conv_weight.at[SELF]), (conv_weight_in.at[SELF], conv_weight.at[G]),
            )
        )
    ]
    for load in loads:
        load.start()

    barrier = pltpu.get_barrier_semaphore()
    for by in OFFSETS:
        pl.semaphore_signal(barrier, inc=1, device_id=device(by), device_id_type=MESH)
    sibling = me + 1 - 2 * core
    pl.semaphore_signal(barrier, inc=1, device_id=(sibling,), device_id_type=MESH)
    for a, b, _ in PLANES:
        for i, j in HOPS:
            if i and j:
                to = me + shift(a, i) + shift(b, j)
                pl.semaphore_signal(barrier, inc=1, device_id=(to,), device_id_type=MESH)
        for i in (1, 2, 3):
            pl.semaphore_signal(barrier, inc=1, device_id=(me + shift(a, i),), device_id_type=MESH)

    def send(src, dst, sems, to):
        return pltpu.make_async_remote_copy(
            src_ref=src, dst_ref=dst, send_sem=sems[0], recv_sem=sems[1], device_id=(to,), device_id_type=MESH
        )

    flying = []

    def start_all(moves, whole, sems):
        for move in moves:
            move.start()
        group = send(whole, whole, sems, sibling)
        flying.append(group)
        return group

    def copies(which, src, dst, sign):
        sems = (send_sem.at[which], recv_sem.at[which])
        moves = [send(src.at[s], dst.at[s], sems, device(sign * OFFSETS[s])) for s in range(S)]
        return start_all(moves, src, sems)

    sums = [None] * 3

    def put_block(block, value):
        part = 0 if block < 16 else 1 if block < 28 else 2
        at = block - (0, 16, 28)[part]
        per_half = CHUNK[part] // 8
        terms[part, at // per_half, pl.ds(at % per_half * C, C), :] = value


    def sum_turn(turn, parts):
        for part in parts:
            if turn:
                sums[part].wait_recv()
            if turn < 5:
                sums[part] = sum_step(turn, part)

    def sum_step(turn, part):
        a, b, c = PLANES[part]
        size = CHUNK[part]
        here = place[a] * 4 + place[b]
        half = pl.ds(0, 16 * size)
        chunk = pl.ds(0, size)
        owned = pl.ds(pl.multiple_of(core * (16 * size) + here * size, 16), size)
        sems = (sum_send.at[turn, part], sum_recv.at[turn, part])
        fifteen = got_plane.at[part, :, chunk]
        if turn == 0:
            mine = terms.at[part, 1 - core, half]
            return start_all([send(mine, got_core.at[part, half], sems, sibling)], mine, sems)
        if turn == 1:
            total = (terms[part, core, half].astype(F32) + got_core[part, half].astype(F32)).astype(BF)
            for q in range(16):
                core_sum[part, q, chunk] = total[q * size : (q + 1) * size]
            moves = [
                send(
                    core_sum.at[part, lax.rem(place[a] + i, 4) * 4 + lax.rem(place[b] + j, 4), chunk],
                    got_plane.at[part, at, chunk], sems, me + shift(a, i) + shift(b, j),
                )
                for at, (i, j) in enumerate(HOPS)
            ]
            return start_all(moves, fifteen, sems)
        if turn == 2:
            total = core_sum[part, here, chunk].astype(F32)
            for at in range(15):
                total += got_plane[part, at, chunk].astype(F32)
            plane_sum[part, place[c], chunk] = total
            mine = plane_sum.at[part, place[c], chunk]
            moves = [send(mine, mine, sems, me + shift(c, i)) for i in (1, 2, 3)]
            return start_all(moves, plane_sum.at[part, pl.ds(0, 3), chunk], sems)
        if turn == 3:
            total = plane_sum[part, 0, chunk] + plane_sum[part, 1, chunk]
            total += plane_sum[part, 2, chunk] + plane_sum[part, 3, chunk]
            summed[part, owned] = total.astype(BF)
            mine = summed.at[part, owned]
            moves = [send(mine, mine, sems, me + shift(a, i) + shift(b, j)) for i, j in HOPS]
            return start_all(moves, fifteen, sems)
        mine = summed.at[part, pl.ds(pl.multiple_of(core * (16 * size), 16), 16 * size)]
        return start_all([send(mine, mine, sems, sibling)], mine, sems)

    loads[0].wait()
    loads[1].wait()
    chosen = t_dot(list_matrix(halo_rows[...], CAP), features[...]).astype(BF)
    for s in range(S):
        out_x[s] = chosen[s * CAP : (s + 1) * CAP]
    table[0:HALF, 0:C] = features[0:HALF, :]
    table[0:HALF, C : 2 * C] = features[HALF:V, :]

    loads[2].wait()
    codes = row_codes(neighbour_map[...], V + S * CAP, True)
    codes_x[0:K, :] = codes
    codes_x[SELF : SELF + 1, :] = codes[G:K, :]
    codes_x[G:32, :] = jnp.zeros((32 - G, V), F32)
    turned_codes = codes_x[...].T.astype(BF)
    for k in range(0, G, 2):
        wide = dot(turned_codes, unit_rows(32, k, 2)).astype(BF)
        for i in range(2):
            wide_x[k + i] = wide[:, i * 128 : (i + 1) * 128]
    pl.semaphore_wait(barrier, S + 37)
    send_x = copies(0, out_x, in_x, 1)

    for load in loads[3:]:
        load.wait()
    rows = child_map[...]
    plain = jnp.where(rows >= V + S * CAP2, 0, ((rows & 127) + 128) << (rows >> 7)).astype(F32)
    for o in range(O):
        total = dot(spread_matrix(plain[o : o + 1, :], 0, V + S * CAP2), out_grad[...]).astype(BF)
        spread_h[:, o * C2 : (o + 1) * C2] = total[0:V]
        for s in range(S):
            out_spread[s, :, o * C2 : (o + 1) * C2] = total[V + s * CAP2 : V + (s + 1) * CAP2]
    send_spread = copies(1, out_spread, in_spread, -1)
    total = jnp.zeros((V, C), F32)
    for o in range(O):
        total += dot_t(spread_h[:, o * C2 : (o + 1) * C2], down_weight[o])
    hidden_grad[...] = total
    def pick_local(step, carry):
        for i in range(3):
            k = step * 3 + i
            z_all[k] = dot(pick_matrix(wide_x[k], 0, 4), table[0:HALF, :]).astype(BF)
        return carry

    lax.fori_loop(0, EARLY, pick_local, 0)
    pre[...] = dot(features[...], conv_weight[G])
    send_x.wait_recv()
    for s in range(S):
        table[pl.ds(HALF + (s % 2) * CAP, CAP), pl.ds((s // 2) * C, C)] = in_x[s]

    def multiply(k, group):
        weights = conv_weight[pl.ds(k, len(group))].reshape(len(group) * C, C)
        pre[...] += dot(jnp.concatenate(group, axis=1), weights)

    def forward_early(step, carry):
        group = []
        for i in range(3):
            k = step * 3 + i
            codes = wide_x[k]
            both = dot(pick_matrix(codes, 4, 5), table[HALF:PAIRS, :]).astype(BF) + z_all[k]
            rows = jnp.where(codes < 0, both[:, C:], both[:, :C])
            picked[k] = rows
            group.append(rows)
        multiply(step * 3, group)
        return carry

    lax.fori_loop(0, EARLY, forward_early, 0)

    def forward(step, carry):
        first = EARLY * 3 + step * 4
        group = []
        for i in range(4):
            codes = wide_x[first + i]
            rows = pick_side(dot(pick_matrix(codes), table[...]), codes)
            picked[first + i] = rows
            group.append(rows)
        multiply(first, group)
        return carry

    lax.fori_loop(0, (G - EARLY * 3) // 4, forward, 0)

    act = pre[...]
    gate = jax.nn.sigmoid(act)
    hidden[...] = (features[...].astype(F32) + act * gate).astype(BF)
    child_pick = list_matrix(child_rows[...], CAP2)
    chosen = t_dot(child_pick, hidden[...]).astype(BF)
    for s in range(S):
        out_h[s] = chosen[s * CAP2 : (s + 1) * CAP2]
    send_h = copies(2, out_h, in_h, 1)
    send_spread.wait_recv()
    turned_hidden = hidden[...].T
    turned_chosen = chosen.T
    for o in range(O):
        at = slice(o * C2, (o + 1) * C2)
        back_spread = jnp.concatenate([in_spread[s, :, at] for s in range(S)], axis=0)
        products = (dot(turned_hidden, spread_h[:, at]) + dot(turned_chosen, back_spread)).astype(BF)
        put_block(28 + 2 * o, products[:, 0:C])
        put_block(29 + 2 * o, products[:, C : 2 * C])
    sum_turn(0, (2,))

    returned = jnp.zeros((S * CAP2, C), F32)
    for o in range(O):
        back_spread = jnp.concatenate([in_spread[s, :, o * C2 : (o + 1) * C2] for s in range(S)], axis=0)
        returned += dot_t(back_spread, down_weight[o])
    grad_h = hidden_grad[...] + dot(child_pick, returned.astype(BF))
    hidden_grad[...] = grad_h
    pre_grad[...] = (grad_h * (gate * (1.0 + act * (1.0 - gate)))).astype(BF)

    turned_grad = pre_grad[...].T
    put_block(SELF, t_dot(features[...], pre_grad[...]).astype(BF))
    for k in range(0, G, 2):
        products = dot(turned_grad, jnp.concatenate([picked[k], picked[k + 1]], axis=1))
        for i in range(2):
            put_block(G if k + i == SELF else k + i, products[:, i * C : (i + 1) * C].T.astype(BF))
        if k == 14:
            sum_turn(0, (0,))
            sum_turn(1, (2,))
    put_block(K, jnp.zeros((C, C), BF))
    sum_turn(0, (1,))
    sum_turn(1, (0,))

    back_x[...] = jnp.zeros_like(back_x)

    def backward_group(first, count):
        weights = conv_weight[pl.ds(first, count)].reshape(count * C, C)
        z = dot_t(pre_grad[...], weights).astype(BF)
        total = back_x[HALF:PAIRS, :]
        for i in range(count):
            z2 = two_sides(z[:, i * C : (i + 1) * C], wide_x[first + i])
            z_all[first + i] = z2
            total += dot(spread_matrix(codes_x[pl.ds(first + i, 1), :], HALF, 128), z2)
        back_x[HALF:PAIRS, :] = total

    def backward(step, carry):
        backward_group(step * 4, 4)
        return carry

    backward_group(G - 2, 2)
    sum_turn(1, (1,))
    lax.fori_loop(0, G // 4, backward, 0)
    for s in range(S):
        out_gx[s] = back_x[pl.ds(HALF + (s % 2) * CAP, CAP), pl.ds((s // 2) * C, C)].astype(BF)
    send_gx = copies(3, out_gx, in_gx, -1)

    def backward_local_group(first, count):
        total = back_x[0:HALF, :]
        for i in range(count):
            total += dot(spread_matrix(codes_x[pl.ds(first + i, 1), :], 0, HALF), z_all[first + i])
        back_x[0:HALF, :] = total

    def backward_local(step, carry):
        backward_local_group(step * 4, 4)
        return carry

    sum_turn(2, (2, 0, 1))
    lax.fori_loop(0, LOCAL_FIRST, backward_local, 0)
    sum_turn(3, (2, 0, 1))

    turned_codes = row_codes(child_map[...], V + S * CAP2, False).T.astype(BF)
    for o in range(0, O, 2):
        wide = dot(turned_codes, unit_rows(O, o, 2)).astype(BF)
        for i in range(2):
            wide_h[pl.ds((o + i) * PD, PD), :] = wide[:, i * 128 : (i + 1) * 128]
    table[0:HALF, 0:C] = hidden[0:HALF, :]
    table[0:HALF, C : 2 * C] = hidden[HALF:V, :]
    table[HALF:PAIRS, C : 2 * C] = jnp.zeros((128, C), BF)
    send_h.wait_recv()
    for s in range(S):
        table[pl.ds(HALF + s * CAP2, CAP2), 0:C] = in_h[s]
    total = jnp.zeros((PD, C2), F32)
    for o in range(O):
        codes = wide_h[pl.ds(o * PD, PD), :]
        rows = pick_side(dot(pick_matrix(codes), table[...]), codes)
        total += dot(rows, down_weight[o])
    coarse[...] = total.astype(BF)


    lax.fori_loop(LOCAL_FIRST, G // 4, backward_local, 0)
    backward_local_group(G - 2, 2)
    hidden_grad[...] += dot_t(pre_grad[...], conv_weight[G])

    send_gx.wait_recv()
    returned = dot(list_matrix(halo_rows[...], CAP), jnp.concatenate([in_gx[s] for s in range(S)], axis=0))
    local_back = jnp.concatenate([back_x[0:HALF, 0:C], back_x[0:HALF, C : 2 * C]], axis=0)
    input_grad[...] = hidden_grad[...] + local_back + returned

    sum_turn(4, (2, 0, 1))
    sum_turn(5, (2, 0, 1))
    for group in flying:
        group.wait_send()


FINISH = [(0, a, a + 4) for a in (0, 4, 8, 12)] + [(1, 0, 4), (1, 4, 8), (1, 8, 11)] + [(2, a, a + 4) for a in (0, 4, 8, 12)]


def finish(
    grad_scale, coarse_in, input_grad_in, summed, coarse, input_grad, conv_grad, down_grad, conv_held, down_held, out_sems
):
    stores = []

    def store(held, out):
        stores.append(pltpu.make_async_copy(held, out, out_sems.at[len(stores)]))
        stores[-1].start()

    store(input_grad_in, input_grad)
    store(coarse_in, coarse)
    for part, first, end in FINISH:
        for block in range(first, end):
            value = summed[part, block * C : (block + 1) * C, :].astype(F32) * grad_scale
            if part < 2:
                conv_held[part * 16 + block] = value
            else:
                down_held[block // 2, :, block % 2 * C : (block % 2 + 1) * C] = value
        if part < 2:
            rows = pl.ds(part * 16 + first, end - first)
            store(conv_held.at[rows], conv_grad.at[rows])
        else:
            rows = pl.ds(first // 2, (end - first) // 2)
            store(down_held.at[rows], down_grad.at[rows])
    for copy in stores:
        copy.wait()


def local(features, conv_weight, down_weight, neighbour_map, halo_rows, child_map, child_rows, out_grad):
    devices = lax.axis_size("shard")
    inputs = (features, conv_weight, down_weight, neighbour_map, halo_rows, child_map, child_rows, out_grad)
    coarse, input_grad, summed = pl.pallas_call(
        kernel,
        out_shape=(
            pltpu.VMEM((PD, C2), BF),
            pltpu.VMEM((V, C), F32),
            pltpu.VMEM((3, 2048, C), BF),
        ),
        in_specs=[pl.BlockSpec(memory_space=pl.ANY)] * 8,
        out_specs=[pl.BlockSpec(memory_space=pltpu.VMEM)] * 3,
        scratch_shapes=[pltpu.VMEM(value.shape, value.dtype) for value in inputs] + [
            pltpu.SemaphoreType.DMA((11,)),
            pltpu.VMEM((32, V), F32),
            pltpu.VMEM((G, V, 128), BF),
            pltpu.VMEM((O * PD, 128), BF),
            pltpu.VMEM((G, V, C), BF),
            pltpu.VMEM((PAIRS, 2 * C), BF),
            pltpu.VMEM((V, C), F32),
            pltpu.VMEM((V, C), BF),
            pltpu.VMEM((V, C), F32),
            pltpu.VMEM((V, C), BF),
            pltpu.VMEM((G, V, 2 * C), BF),
            pltpu.VMEM((PAIRS, 2 * C), F32),
            pltpu.VMEM((V, O * C2), BF),
            pltpu.VMEM((S, CAP, C), BF),
            pltpu.VMEM((S, CAP, C), BF),
            pltpu.VMEM((S, CAP2, C), BF),
            pltpu.VMEM((S, CAP2, C), BF),
            pltpu.VMEM((S, CAP2, O * C2), BF),
            pltpu.VMEM((S, CAP2, O * C2), BF),
            pltpu.VMEM((S, CAP, C), BF),
            pltpu.VMEM((S, CAP, C), BF),
            pltpu.SemaphoreType.DMA((4,)),
            pltpu.SemaphoreType.DMA((4,)),
            pltpu.VMEM((3, 2, 1024, C), BF),
            pltpu.VMEM((3, 1024, C), BF),
            pltpu.VMEM((3, 16, 64, C), BF),
            pltpu.VMEM((3, 15, 64, C), BF),
            pltpu.VMEM((3, 4, 64, C), F32),
            pltpu.SemaphoreType.DMA((5, 3)),
            pltpu.SemaphoreType.DMA((5, 3)),
        ],
        compiler_params=pltpu.CompilerParams(
            collective_id=0, has_side_effects=True, vmem_limit_bytes=52 * 2**20
        ),
    )(*inputs)
    grad_scale = 1.0 / math.sqrt(V * devices)
    return pl.pallas_call(
        lambda *refs: finish(grad_scale, *refs),
        out_shape=(
            jax.ShapeDtypeStruct((PD, C2), BF),
            jax.ShapeDtypeStruct((V, C), F32),
            jax.ShapeDtypeStruct((K, C, C), F32),
            jax.ShapeDtypeStruct((O, C, C2), F32),
        ),
        in_specs=[pl.BlockSpec(memory_space=pltpu.VMEM)] * 3,
        out_specs=[pl.BlockSpec(memory_space=pl.ANY)] * 4,
        scratch_shapes=[
            pltpu.VMEM((K, C, C), F32),
            pltpu.VMEM((O, C, C2), F32),
            pltpu.SemaphoreType.DMA((len(FINISH) + 2,)),
        ],
        compiler_params=pltpu.CompilerParams(vmem_limit_bytes=52 * 2**20),
    )(*[pltpu.with_memory_space_constraint(value, pltpu.VMEM) for value in (coarse, input_grad, summed)])


def solution(mesh):
    return jax.shard_map(
        local,
        mesh=mesh,
        in_specs=(
            P("shard", None),
            P(),
            P(),
            P(None, "shard"),
            P(None, "shard"),
            P(None, "shard"),
            P(None, "shard"),
            P("shard", None),
        ),
        out_specs=(P("shard", None), P("shard", None), P(), P()),
        check_vma=False,
    )
```

```python
import math

import jax
import jax.numpy as jnp
from jax import lax
from jax.experimental import pallas as pl
from jax.experimental.pallas import tpu as pltpu
from jax.sharding import PartitionSpec as P

MESH = pl.DeviceIdType.MESH
BF = jnp.bfloat16
F32 = jnp.float32
K = 27
SELF = 13
G = K - 1
O = 8
V = 1024
PD = 256
C = 128
C2 = 256
S = 4
CAP = 64
CAP2 = 32
HALF = V // 2
PAIRS = HALF + 128
OFFSETS = (-2, -1, 1, 2)
LOCAL_FIRST = 3
EARLY = 1
PLANES = ((2, 8, 32), (8, 32, 2), (32, 2, 8))
CHUNK = (64, 48, 64)
HOPS = [(i, j) for i in (2, 1, 3, 0) for j in (2, 1, 3, 0) if i or j]


def row_codes(rows, last, fold_received):
    received = rows >= V
    in_received = (rows >> 7) & 1 if fold_received else jnp.zeros_like(rows)
    side = jnp.where(received, in_received, (rows >> 9) & 1)
    block = jnp.where(received, 4, (rows >> 7) & 3)
    code = ((rows & 127) + 128) << block
    code = jnp.where(side == 1, -code, code)
    return jnp.where(rows >= last, 0, code).astype(F32)


def table_codes(shape, dim, start=0):
    place = lax.broadcasted_iota(jnp.int32, shape, dim) + start
    return (((place & 127) + 128) << (place >> 7)).astype(F32).astype(BF)


def pick_matrix(codes, first=0, end=PAIRS // 128):
    size = jnp.abs(codes)
    names = table_codes((1, PAIRS), 1)
    one, zero = jnp.ones((), BF), jnp.zeros((), BF)
    return jnp.concatenate(
        [jnp.where(size == names[:, b * 128 : (b + 1) * 128], one, zero) for b in range(first, end)], axis=1
    )


def spread_matrix(row, start, count):
    n = row.shape[1]
    size = jnp.broadcast_to(jnp.abs(row), (count, n)).astype(BF)
    names = table_codes((count, 128), 0, start)
    names = jnp.concatenate([names] * (n // 128), axis=1)
    return jnp.where(size == names, jnp.ones((), BF), jnp.zeros((), BF))


def pick_side(both, codes):
    both = both.astype(BF)
    return jnp.where(codes < 0, both[:, C:], both[:, :C])


def two_sides(rows, codes):
    zero = jnp.zeros((), BF)
    return jnp.concatenate([jnp.where(codes >= 0, rows, zero), jnp.where(codes < 0, rows, zero)], axis=1)


def dot(a, b):
    return jnp.dot(a, b, preferred_element_type=F32)


def dot_t(a, b):
    return lax.dot_general(a, b, (((1,), (1,)), ((), ())), preferred_element_type=F32)


def t_dot(a, b):
    return lax.dot_general(a, b, (((0,), (0,)), ((), ())), preferred_element_type=F32)


def unit_rows(rows, first, count):
    at = lax.broadcasted_iota(jnp.int32, (rows, 128 * count), 0)
    block = lax.broadcasted_iota(jnp.int32, (rows, 128 * count), 1) >> 7
    return (at == block + first).astype(F32).astype(BF)


def list_matrix(lists, cap):
    row = jnp.concatenate([lists[s : s + 1, :] for s in range(S)], axis=1)
    places = lax.broadcasted_iota(jnp.int32, (V, S * cap), 0)
    return (places == row).astype(F32).astype(BF)


def kernel(
    features_in, conv_weight_in, down_weight_in, neighbour_map_in, halo_rows_in, child_map_in, child_rows_in, out_grad_in,
    coarse, input_grad, summed,
    features, conv_weight, down_weight, neighbour_map, halo_rows, child_map, child_rows, out_grad, in_sems,
    codes_x, wide_x, wide_h, picked, table, pre, hidden, hidden_grad, pre_grad, z_all, back_x, spread_h,
    out_x, in_x, out_h, in_h, out_spread, in_spread, out_gx, in_gx, send_sem, recv_sem,
    terms, got_core, core_sum, got_plane, plane_sum,
    sum_send, sum_recv,
):
    n = lax.axis_size("shard")
    me = lax.axis_index("shard")
    core = lax.rem(me, 2)
    place = {stride: lax.rem(me // stride, 4) for stride in (2, 8, 32)}

    def shift(stride, by):
        return (lax.rem(place[stride] + by, 4) - place[stride]) * stride

    def device(by):
        return (lax.rem(me + by + n, n),)

    loads = [
        pltpu.make_async_copy(src, dst, in_sems.at[at])
        for at, (src, dst) in enumerate(
            (
                (halo_rows_in, halo_rows), (features_in, features), (neighbour_map_in, neighbour_map),
                (child_map_in, child_map), (out_grad_in, out_grad), (down_weight_in, down_weight),
                (child_rows_in, child_rows),
                (conv_weight_in.at[pl.ds(0, SELF)], conv_weight.at[pl.ds(0, SELF)]),
                (conv_weight_in.at[pl.ds(SELF + 1, G - SELF - 1)], conv_weight.at[pl.ds(SELF + 1, G - SELF - 1)]),
                (conv_weight_in.at[G], conv_weight.at[SELF]), (conv_weight_in.at[SELF], conv_weight.at[G]),
            )
        )
    ]
    for load in loads:
        load.start()

    barrier = pltpu.get_barrier_semaphore()
    for by in OFFSETS:
        pl.semaphore_signal(barrier, inc=1, device_id=device(by), device_id_type=MESH)
    sibling = me + 1 - 2 * core
    pl.semaphore_signal(barrier, inc=1, device_id=(sibling,), device_id_type=MESH)
    for a, b, _ in PLANES:
        for i, j in HOPS:
            if i and j:
                to = me + shift(a, i) + shift(b, j)
                pl.semaphore_signal(barrier, inc=1, device_id=(to,), device_id_type=MESH)
        for i in (1, 2, 3):
            pl.semaphore_signal(barrier, inc=1, device_id=(me + shift(a, i),), device_id_type=MESH)

    def send(src, dst, sems, to):
        return pltpu.make_async_remote_copy(
            src_ref=src, dst_ref=dst, send_sem=sems[0], recv_sem=sems[1], device_id=(to,), device_id_type=MESH
        )

    flying = []

    def start_all(moves, whole, sems):
        for move in moves:
            move.start()
        group = send(whole, whole, sems, sibling)
        flying.append(group)
        return group

    def copies(which, src, dst, sign):
        sems = (send_sem.at[which], recv_sem.at[which])
        moves = [send(src.at[s], dst.at[s], sems, device(sign * OFFSETS[s])) for s in range(S)]
        return start_all(moves, src, sems)

    sums = [None] * 3

    def put_block(block, value):
        part = 0 if block < 16 else 1 if block < 28 else 2
        at = block - (0, 16, 28)[part]
        per_half = CHUNK[part] // 8
        terms[part, at // per_half, pl.ds(at % per_half * C, C), :] = value


    def sum_turn(turn, parts):
        for part in parts:
            if turn:
                sums[part].wait_recv()
            if turn < 5:
                sums[part] = sum_step(turn, part)

    def sum_step(turn, part):
        a, b, c = PLANES[part]
        size = CHUNK[part]
        here = place[a] * 4 + place[b]
        half = pl.ds(0, 16 * size)
        chunk = pl.ds(0, size)
        owned = pl.ds(pl.multiple_of(core * (16 * size) + here * size, 16), size)
        sems = (sum_send.at[turn, part], sum_recv.at[turn, part])
        fifteen = got_plane.at[part, :, chunk]
        if turn == 0:
            mine = terms.at[part, 1 - core, half]
            return start_all([send(mine, got_core.at[part, half], sems, sibling)], mine, sems)
        if turn == 1:
            total = (terms[part, core, half].astype(F32) + got_core[part, half].astype(F32)).astype(BF)
            for q in range(16):
                core_sum[part, q, chunk] = total[q * size : (q + 1) * size]
            moves = [
                send(
                    core_sum.at[part, lax.rem(place[a] + i, 4) * 4 + lax.rem(place[b] + j, 4), chunk],
                    got_plane.at[part, at, chunk], sems, me + shift(a, i) + shift(b, j),
                )
                for at, (i, j) in enumerate(HOPS)
            ]
            return start_all(moves, fifteen, sems)
        if turn == 2:
            total = core_sum[part, here, chunk].astype(F32)
            for at in range(15):
                total += got_plane[part, at, chunk].astype(F32)
            plane_sum[part, place[c], chunk] = total
            mine = plane_sum.at[part, place[c], chunk]
            moves = [send(mine, mine, sems, me + shift(c, i)) for i in (1, 2, 3)]
            return start_all(moves, plane_sum.at[part, pl.ds(0, 3), chunk], sems)
        if turn == 3:
            total = plane_sum[part, 0, chunk] + plane_sum[part, 1, chunk]
            total += plane_sum[part, 2, chunk] + plane_sum[part, 3, chunk]
            summed[part, owned] = total.astype(BF)
            mine = summed.at[part, owned]
            moves = [send(mine, mine, sems, me + shift(a, i) + shift(b, j)) for i, j in HOPS]
            return start_all(moves, fifteen, sems)
        mine = summed.at[part, pl.ds(pl.multiple_of(core * (16 * size), 16), 16 * size)]
        return start_all([send(mine, mine, sems, sibling)], mine, sems)

    loads[0].wait()
    loads[1].wait()
    chosen = t_dot(list_matrix(halo_rows[...], CAP), features[...]).astype(BF)
    for s in range(S):
        out_x[s] = chosen[s * CAP : (s + 1) * CAP]
    table[0:HALF, 0:C] = features[0:HALF, :]
    table[0:HALF, C : 2 * C] = features[HALF:V, :]

    loads[2].wait()
    codes = row_codes(neighbour_map[...], V + S * CAP, True)
    codes_x[0:K, :] = codes
    codes_x[SELF : SELF + 1, :] = codes[G:K, :]
    codes_x[G:32, :] = jnp.zeros((32 - G, V), F32)
    turned_codes = codes_x[...].T.astype(BF)
    for k in range(0, G, 2):
        wide = dot(turned_codes, unit_rows(32, k, 2)).astype(BF)
        for i in range(2):
            wide_x[k + i] = wide[:, i * 128 : (i + 1) * 128]
    pl.semaphore_wait(barrier, S + 37)
    send_x = copies(0, out_x, in_x, 1)

    for load in loads[3:]:
        load.wait()
    rows = child_map[...]
    plain = jnp.where(rows >= V + S * CAP2, 0, ((rows & 127) + 128) << (rows >> 7)).astype(F32)
    for o in range(O):
        total = dot(spread_matrix(plain[o : o + 1, :], 0, V + S * CAP2), out_grad[...]).astype(BF)
        spread_h[:, o * C2 : (o + 1) * C2] = total[0:V]
        for s in range(S):
            out_spread[s, :, o * C2 : (o + 1) * C2] = total[V + s * CAP2 : V + (s + 1) * CAP2]
    send_spread = copies(1, out_spread, in_spread, -1)
    total = jnp.zeros((V, C), F32)
    for o in range(O):
        total += dot_t(spread_h[:, o * C2 : (o + 1) * C2], down_weight[o])
    hidden_grad[...] = total
    def pick_local(step, carry):
        for i in range(2):
            k = step * 2 + i
            z_all[k] = dot(pick_matrix(wide_x[k], 0, 4), table[0:HALF, :]).astype(BF)
        return carry

    lax.fori_loop(0, EARLY, pick_local, 0)
    pre[...] = dot(features[...], conv_weight[G])
    send_x.wait_recv()
    for s in range(S):
        table[pl.ds(HALF + (s % 2) * CAP, CAP), pl.ds((s // 2) * C, C)] = in_x[s]

    def multiply(k, group):
        weights = conv_weight[pl.ds(k, len(group))].reshape(len(group) * C, C)
        pre[...] += dot(jnp.concatenate(group, axis=1), weights)

    def forward_early(step, carry):
        group = []
        for i in range(2):
            k = step * 2 + i
            codes = wide_x[k]
            both = dot(pick_matrix(codes, 4, 5), table[HALF:PAIRS, :]).astype(BF) + z_all[k]
            rows = jnp.where(codes < 0, both[:, C:], both[:, :C])
            picked[k] = rows
            group.append(rows)
        multiply(step * 2, group)
        return carry

    lax.fori_loop(0, EARLY, forward_early, 0)

    def forward(step, carry):
        first = EARLY * 2 + step * 6
        group = []
        for i in range(6):
            codes = wide_x[first + i]
            rows = pick_side(dot(pick_matrix(codes), table[...]), codes)
            picked[first + i] = rows
            group.append(rows)
        multiply(first, group)
        return carry

    lax.fori_loop(0, (G - EARLY * 2) // 6, forward, 0)

    act = pre[...]
    gate = jax.nn.sigmoid(act)
    hidden[...] = (features[...].astype(F32) + act * gate).astype(BF)
    child_pick = list_matrix(child_rows[...], CAP2)
    chosen = t_dot(child_pick, hidden[...]).astype(BF)
    for s in range(S):
        out_h[s] = chosen[s * CAP2 : (s + 1) * CAP2]
    send_h = copies(2, out_h, in_h, 1)
    send_spread.wait_recv()
    turned_hidden = hidden[...].T
    turned_chosen = chosen.T
    for o in range(O):
        at = slice(o * C2, (o + 1) * C2)
        back_spread = jnp.concatenate([in_spread[s, :, at] for s in range(S)], axis=0)
        products = (dot(turned_hidden, spread_h[:, at]) + dot(turned_chosen, back_spread)).astype(BF)
        put_block(28 + 2 * o, products[:, 0:C])
        put_block(29 + 2 * o, products[:, C : 2 * C])
    sum_turn(0, (2,))

    returned = jnp.zeros((S * CAP2, C), F32)
    for o in range(O):
        back_spread = jnp.concatenate([in_spread[s, :, o * C2 : (o + 1) * C2] for s in range(S)], axis=0)
        returned += dot_t(back_spread, down_weight[o])
    grad_h = hidden_grad[...] + dot(child_pick, returned.astype(BF))
    hidden_grad[...] = grad_h
    pre_grad[...] = (grad_h * (gate * (1.0 + act * (1.0 - gate)))).astype(BF)

    turned_grad = pre_grad[...].T
    put_block(SELF, t_dot(features[...], pre_grad[...]).astype(BF))
    for k in range(0, G, 2):
        products = dot(turned_grad, jnp.concatenate([picked[k], picked[k + 1]], axis=1))
        for i in range(2):
            put_block(G if k + i == SELF else k + i, products[:, i * C : (i + 1) * C].T.astype(BF))
        if k == 14:
            sum_turn(0, (0,))
            sum_turn(1, (2,))
    put_block(K, jnp.zeros((C, C), BF))
    sum_turn(0, (1,))
    sum_turn(1, (0,))

    back_x[...] = jnp.zeros_like(back_x)

    def backward_group(first, count):
        weights = conv_weight[pl.ds(first, count)].reshape(count * C, C)
        z = dot_t(pre_grad[...], weights).astype(BF)
        total = back_x[HALF:PAIRS, :]
        for i in range(count):
            z2 = two_sides(z[:, i * C : (i + 1) * C], wide_x[first + i])
            z_all[first + i] = z2
            total += dot(spread_matrix(codes_x[pl.ds(first + i, 1), :], HALF, 128), z2)
        back_x[HALF:PAIRS, :] = total

    def backward(step, carry):
        backward_group(step * 4, 4)
        return carry

    backward_group(G - 2, 2)
    sum_turn(1, (1,))
    lax.fori_loop(0, G // 4, backward, 0)
    for s in range(S):
        out_gx[s] = back_x[pl.ds(HALF + (s % 2) * CAP, CAP), pl.ds((s // 2) * C, C)].astype(BF)
    send_gx = copies(3, out_gx, in_gx, -1)

    def backward_local_group(first, count):
        total = back_x[0:HALF, :]
        for i in range(count):
            total += dot(spread_matrix(codes_x[pl.ds(first + i, 1), :], 0, HALF), z_all[first + i])
        back_x[0:HALF, :] = total

    def backward_local(step, carry):
        backward_local_group(step * 4, 4)
        return carry

    sum_turn(2, (2, 0, 1))
    lax.fori_loop(0, LOCAL_FIRST, backward_local, 0)
    sum_turn(3, (2, 0, 1))

    turned_codes = row_codes(child_map[...], V + S * CAP2, False).T.astype(BF)
    for o in range(0, O, 2):
        wide = dot(turned_codes, unit_rows(O, o, 2)).astype(BF)
        for i in range(2):
            wide_h[pl.ds((o + i) * PD, PD), :] = wide[:, i * 128 : (i + 1) * 128]
    table[0:HALF, 0:C] = hidden[0:HALF, :]
    table[0:HALF, C : 2 * C] = hidden[HALF:V, :]
    table[HALF:PAIRS, C : 2 * C] = jnp.zeros((128, C), BF)
    send_h.wait_recv()
    for s in range(S):
        table[pl.ds(HALF + s * CAP2, CAP2), 0:C] = in_h[s]
    total = jnp.zeros((PD, C2), F32)
    for o in range(O):
        codes = wide_h[pl.ds(o * PD, PD), :]
        rows = pick_side(dot(pick_matrix(codes), table[...]), codes)
        total += dot(rows, down_weight[o])
    coarse[...] = total.astype(BF)


    lax.fori_loop(LOCAL_FIRST, G // 4, backward_local, 0)
    backward_local_group(G - 2, 2)
    hidden_grad[...] += dot_t(pre_grad[...], conv_weight[G])

    send_gx.wait_recv()
    returned = dot(list_matrix(halo_rows[...], CAP), jnp.concatenate([in_gx[s] for s in range(S)], axis=0))
    local_back = jnp.concatenate([back_x[0:HALF, 0:C], back_x[0:HALF, C : 2 * C]], axis=0)
    input_grad[...] = hidden_grad[...] + local_back + returned

    sum_turn(4, (2, 0, 1))
    sum_turn(5, (2, 0, 1))
    for group in flying:
        group.wait_send()


FINISH = [(0, a, a + 4) for a in (0, 4, 8, 12)] + [(1, 0, 4), (1, 4, 8), (1, 8, 11)] + [(2, a, a + 4) for a in (0, 4, 8, 12)]


def finish(
    grad_scale, coarse_in, input_grad_in, summed, coarse, input_grad, conv_grad, down_grad, conv_held, down_held, out_sems
):
    stores = []

    def store(held, out):
        stores.append(pltpu.make_async_copy(held, out, out_sems.at[len(stores)]))
        stores[-1].start()

    store(input_grad_in, input_grad)
    store(coarse_in, coarse)
    for part, first, end in FINISH:
        for block in range(first, end):
            value = summed[part, block * C : (block + 1) * C, :].astype(F32) * grad_scale
            if part < 2:
                conv_held[part * 16 + block] = value
            else:
                down_held[block // 2, :, block % 2 * C : (block % 2 + 1) * C] = value
        if part < 2:
            rows = pl.ds(part * 16 + first, end - first)
            store(conv_held.at[rows], conv_grad.at[rows])
        else:
            rows = pl.ds(first // 2, (end - first) // 2)
            store(down_held.at[rows], down_grad.at[rows])
    for copy in stores:
        copy.wait()


def local(features, conv_weight, down_weight, neighbour_map, halo_rows, child_map, child_rows, out_grad):
    devices = lax.axis_size("shard")
    inputs = (features, conv_weight, down_weight, neighbour_map, halo_rows, child_map, child_rows, out_grad)
    coarse, input_grad, summed = pl.pallas_call(
        kernel,
        out_shape=(
            pltpu.VMEM((PD, C2), BF),
            pltpu.VMEM((V, C), F32),
            pltpu.VMEM((3, 2048, C), BF),
        ),
        in_specs=[pl.BlockSpec(memory_space=pl.ANY)] * 8,
        out_specs=[pl.BlockSpec(memory_space=pltpu.VMEM)] * 3,
        scratch_shapes=[pltpu.VMEM(value.shape, value.dtype) for value in inputs] + [
            pltpu.SemaphoreType.DMA((11,)),
            pltpu.VMEM((32, V), F32),
            pltpu.VMEM((G, V, 128), BF),
            pltpu.VMEM((O * PD, 128), BF),
            pltpu.VMEM((G, V, C), BF),
            pltpu.VMEM((PAIRS, 2 * C), BF),
            pltpu.VMEM((V, C), F32),
            pltpu.VMEM((V, C), BF),
            pltpu.VMEM((V, C), F32),
            pltpu.VMEM((V, C), BF),
            pltpu.VMEM((G, V, 2 * C), BF),
            pltpu.VMEM((PAIRS, 2 * C), F32),
            pltpu.VMEM((V, O * C2), BF),
            pltpu.VMEM((S, CAP, C), BF),
            pltpu.VMEM((S, CAP, C), BF),
            pltpu.VMEM((S, CAP2, C), BF),
            pltpu.VMEM((S, CAP2, C), BF),
            pltpu.VMEM((S, CAP2, O * C2), BF),
            pltpu.VMEM((S, CAP2, O * C2), BF),
            pltpu.VMEM((S, CAP, C), BF),
            pltpu.VMEM((S, CAP, C), BF),
            pltpu.SemaphoreType.DMA((4,)),
            pltpu.SemaphoreType.DMA((4,)),
            pltpu.VMEM((3, 2, 1024, C), BF),
            pltpu.VMEM((3, 1024, C), BF),
            pltpu.VMEM((3, 16, 64, C), BF),
            pltpu.VMEM((3, 15, 64, C), BF),
            pltpu.VMEM((3, 4, 64, C), F32),
            pltpu.SemaphoreType.DMA((5, 3)),
            pltpu.SemaphoreType.DMA((5, 3)),
        ],
        compiler_params=pltpu.CompilerParams(
            collective_id=0, has_side_effects=True, vmem_limit_bytes=52 * 2**20
        ),
    )(*inputs)
    grad_scale = 1.0 / math.sqrt(V * devices)
    return pl.pallas_call(
        lambda *refs: finish(grad_scale, *refs),
        out_shape=(
            jax.ShapeDtypeStruct((PD, C2), BF),
            jax.ShapeDtypeStruct((V, C), F32),
            jax.ShapeDtypeStruct((K, C, C), F32),
            jax.ShapeDtypeStruct((O, C, C2), F32),
        ),
        in_specs=[pl.BlockSpec(memory_space=pltpu.VMEM)] * 3,
        out_specs=[pl.BlockSpec(memory_space=pl.ANY)] * 4,
        scratch_shapes=[
            pltpu.VMEM((K, C, C), F32),
            pltpu.VMEM((O, C, C2), F32),
            pltpu.SemaphoreType.DMA((len(FINISH) + 2,)),
        ],
        compiler_params=pltpu.CompilerParams(vmem_limit_bytes=52 * 2**20),
    )(*[pltpu.with_memory_space_constraint(value, pltpu.VMEM) for value in (coarse, input_grad, summed)])


def solution(mesh):
    return jax.shard_map(
        local,
        mesh=mesh,
        in_specs=(
            P("shard", None),
            P(),
            P(),
            P(None, "shard"),
            P(None, "shard"),
            P(None, "shard"),
            P(None, "shard"),
            P("shard", None),
        ),
        out_specs=(P("shard", None), P("shard", None), P(), P()),
        check_vma=False,
    )
```

```python
import math

import jax
import jax.numpy as jnp
from jax import lax
from jax.experimental import pallas as pl
from jax.experimental.pallas import tpu as pltpu
from jax.sharding import PartitionSpec as P

MESH = pl.DeviceIdType.MESH
BF = jnp.bfloat16
F32 = jnp.float32
K = 27
SELF = 13
G = K - 1
O = 8
V = 1024
PD = 256
C = 128
C2 = 256
S = 4
CAP = 64
CAP2 = 32
HALF = V // 2
PAIRS = HALF + 128
OFFSETS = (-2, -1, 1, 2)
LOCAL_FIRST = 3
EARLY = 1
PLANES = ((2, 8, 32), (8, 32, 2), (32, 2, 8))
CHUNK = (64, 48, 64)
HOPS = [(i, j) for i in (2, 1, 3, 0) for j in (2, 1, 3, 0) if i or j]


def row_codes(rows, last, fold_received):
    received = rows >= V
    in_received = (rows >> 7) & 1 if fold_received else jnp.zeros_like(rows)
    side = jnp.where(received, in_received, (rows >> 9) & 1)
    block = jnp.where(received, 4, (rows >> 7) & 3)
    code = ((rows & 127) + 128) << block
    code = jnp.where(side == 1, -code, code)
    return jnp.where(rows >= last, 0, code).astype(F32)


def table_codes(shape, dim, start=0):
    place = lax.broadcasted_iota(jnp.int32, shape, dim) + start
    return (((place & 127) + 128) << (place >> 7)).astype(F32).astype(BF)


def pick_matrix(codes, first=0, end=PAIRS // 128):
    size = jnp.abs(codes)
    names = table_codes((1, PAIRS), 1)
    one, zero = jnp.ones((), BF), jnp.zeros((), BF)
    return jnp.concatenate(
        [jnp.where(size == names[:, b * 128 : (b + 1) * 128], one, zero) for b in range(first, end)], axis=1
    )


def spread_matrix(row, start, count):
    n = row.shape[1]
    size = jnp.broadcast_to(jnp.abs(row), (count, n)).astype(BF)
    names = table_codes((count, 128), 0, start)
    names = jnp.concatenate([names] * (n // 128), axis=1)
    return jnp.where(size == names, jnp.ones((), BF), jnp.zeros((), BF))


def pick_side(both, codes):
    both = both.astype(BF)
    return jnp.where(codes < 0, both[:, C:], both[:, :C])


def two_sides(rows, codes):
    zero = jnp.zeros((), BF)
    return jnp.concatenate([jnp.where(codes >= 0, rows, zero), jnp.where(codes < 0, rows, zero)], axis=1)


def dot(a, b):
    return jnp.dot(a, b, preferred_element_type=F32)


def dot_t(a, b):
    return lax.dot_general(a, b, (((1,), (1,)), ((), ())), preferred_element_type=F32)


def t_dot(a, b):
    return lax.dot_general(a, b, (((0,), (0,)), ((), ())), preferred_element_type=F32)


def unit_rows(rows, first, count):
    at = lax.broadcasted_iota(jnp.int32, (rows, 128 * count), 0)
    block = lax.broadcasted_iota(jnp.int32, (rows, 128 * count), 1) >> 7
    return (at == block + first).astype(F32).astype(BF)


def list_matrix(lists, cap):
    row = jnp.concatenate([lists[s : s + 1, :] for s in range(S)], axis=1)
    places = lax.broadcasted_iota(jnp.int32, (V, S * cap), 0)
    return (places == row).astype(F32).astype(BF)


def kernel(
    features_in, conv_weight_in, down_weight_in, neighbour_map_in, halo_rows_in, child_map_in, child_rows_in, out_grad_in,
    coarse, input_grad, summed,
    features, conv_weight, down_weight, neighbour_map, halo_rows, child_map, child_rows, out_grad, in_sems,
    codes_x, wide_x, wide_h, picked, table, pre, hidden, hidden_grad, pre_grad, z_all, back_x, spread_h,
    out_x, in_x, out_h, in_h, out_spread, in_spread, out_gx, in_gx, send_sem, recv_sem,
    terms, got_core, core_sum, got_plane, plane_sum,
    sum_send, sum_recv, child_pick, turned_features,
):
    n = lax.axis_size("shard")
    me = lax.axis_index("shard")
    core = lax.rem(me, 2)
    place = {stride: lax.rem(me // stride, 4) for stride in (2, 8, 32)}

    def shift(stride, by):
        return (lax.rem(place[stride] + by, 4) - place[stride]) * stride

    def device(by):
        return (lax.rem(me + by + n, n),)

    loads = [
        pltpu.make_async_copy(src, dst, in_sems.at[at])
        for at, (src, dst) in enumerate(
            (
                (halo_rows_in, halo_rows), (features_in, features), (neighbour_map_in, neighbour_map),
                (child_map_in, child_map), (out_grad_in, out_grad), (down_weight_in, down_weight),
                (child_rows_in, child_rows),
                (conv_weight_in.at[pl.ds(0, SELF)], conv_weight.at[pl.ds(0, SELF)]),
                (conv_weight_in.at[pl.ds(SELF + 1, G - SELF - 1)], conv_weight.at[pl.ds(SELF + 1, G - SELF - 1)]),
                (conv_weight_in.at[G], conv_weight.at[SELF]), (conv_weight_in.at[SELF], conv_weight.at[G]),
            )
        )
    ]
    for load in loads:
        load.start()

    barrier = pltpu.get_barrier_semaphore()
    for by in OFFSETS:
        pl.semaphore_signal(barrier, inc=1, device_id=device(by), device_id_type=MESH)
    sibling = me + 1 - 2 * core
    pl.semaphore_signal(barrier, inc=1, device_id=(sibling,), device_id_type=MESH)
    for a, b, _ in PLANES:
        for i, j in HOPS:
            if i and j:
                to = me + shift(a, i) + shift(b, j)
                pl.semaphore_signal(barrier, inc=1, device_id=(to,), device_id_type=MESH)
        for i in (1, 2, 3):
            pl.semaphore_signal(barrier, inc=1, device_id=(me + shift(a, i),), device_id_type=MESH)

    def send(src, dst, sems, to):
        return pltpu.make_async_remote_copy(
            src_ref=src, dst_ref=dst, send_sem=sems[0], recv_sem=sems[1], device_id=(to,), device_id_type=MESH
        )

    flying = []

    def start_all(moves, whole, sems):
        for move in moves:
            move.start()
        group = send(whole, whole, sems, sibling)
        flying.append(group)
        return group

    def copies(which, src, dst, sign):
        sems = (send_sem.at[which], recv_sem.at[which])
        moves = [send(src.at[s], dst.at[s], sems, device(sign * OFFSETS[s])) for s in range(S)]
        return start_all(moves, src, sems)

    sums = [None] * 3

    def put_block(block, value):
        part = 0 if block < 16 else 1 if block < 28 else 2
        at = block - (0, 16, 28)[part]
        per_half = CHUNK[part] // 8
        terms[part, at // per_half, pl.ds(at % per_half * C, C), :] = value


    def sum_turn(turn, parts):
        for part in parts:
            if turn:
                sums[part].wait_recv()
            if turn < 5:
                sums[part] = sum_step(turn, part)

    def sum_step(turn, part):
        a, b, c = PLANES[part]
        size = CHUNK[part]
        here = place[a] * 4 + place[b]
        half = pl.ds(0, 16 * size)
        chunk = pl.ds(0, size)
        owned = pl.ds(pl.multiple_of(core * (16 * size) + here * size, 16), size)
        sems = (sum_send.at[turn, part], sum_recv.at[turn, part])
        fifteen = got_plane.at[part, :, chunk]
        if turn == 0:
            mine = terms.at[part, 1 - core, half]
            return start_all([send(mine, got_core.at[part, half], sems, sibling)], mine, sems)
        if turn == 1:
            total = (terms[part, core, half].astype(F32) + got_core[part, half].astype(F32)).astype(BF)
            for q in range(16):
                core_sum[part, q, chunk] = total[q * size : (q + 1) * size]
            moves = [
                send(
                    core_sum.at[part, lax.rem(place[a] + i, 4) * 4 + lax.rem(place[b] + j, 4), chunk],
                    got_plane.at[part, at, chunk], sems, me + shift(a, i) + shift(b, j),
                )
                for at, (i, j) in enumerate(HOPS)
            ]
            return start_all(moves, fifteen, sems)
        if turn == 2:
            total = core_sum[part, here, chunk].astype(F32)
            for at in range(15):
                total += got_plane[part, at, chunk].astype(F32)
            plane_sum[part, place[c], chunk] = total
            mine = plane_sum.at[part, place[c], chunk]
            moves = [send(mine, mine, sems, me + shift(c, i)) for i in (1, 2, 3)]
            return start_all(moves, plane_sum.at[part, pl.ds(0, 3), chunk], sems)
        if turn == 3:
            total = plane_sum[part, 0, chunk] + plane_sum[part, 1, chunk]
            total += plane_sum[part, 2, chunk] + plane_sum[part, 3, chunk]
            summed[part, owned] = total.astype(BF)
            mine = summed.at[part, owned]
            moves = [send(mine, mine, sems, me + shift(a, i) + shift(b, j)) for i, j in HOPS]
            return start_all(moves, fifteen, sems)
        mine = summed.at[part, pl.ds(pl.multiple_of(core * (16 * size), 16), 16 * size)]
        return start_all([send(mine, mine, sems, sibling)], mine, sems)

    loads[0].wait()
    loads[1].wait()
    chosen = t_dot(list_matrix(halo_rows[...], CAP), features[...]).astype(BF)
    for s in range(S):
        out_x[s] = chosen[s * CAP : (s + 1) * CAP]
    table[0:HALF, 0:C] = features[0:HALF, :]
    table[0:HALF, C : 2 * C] = features[HALF:V, :]

    loads[2].wait()
    codes = row_codes(neighbour_map[...], V + S * CAP, True)
    codes_x[0:K, :] = codes
    codes_x[SELF : SELF + 1, :] = codes[G:K, :]
    codes_x[G:32, :] = jnp.zeros((32 - G, V), F32)
    turned_codes = codes_x[...].T.astype(BF)
    for k in range(0, G, 2):
        wide = dot(turned_codes, unit_rows(32, k, 2)).astype(BF)
        for i in range(2):
            wide_x[k + i] = wide[:, i * 128 : (i + 1) * 128]
    pl.semaphore_wait(barrier, S + 37)
    send_x = copies(0, out_x, in_x, 1)

    for load in loads[3:]:
        load.wait()
    rows = child_map[...]
    plain = jnp.where(rows >= V + S * CAP2, 0, ((rows & 127) + 128) << (rows >> 7)).astype(F32)
    for o in range(O):
        total = dot(spread_matrix(plain[o : o + 1, :], 0, V + S * CAP2), out_grad[...]).astype(BF)
        spread_h[:, o * C2 : (o + 1) * C2] = total[0:V]
        for s in range(S):
            out_spread[s, :, o * C2 : (o + 1) * C2] = total[V + s * CAP2 : V + (s + 1) * CAP2]
    send_spread = copies(1, out_spread, in_spread, -1)
    total = jnp.zeros((V, C), F32)
    for o in range(O):
        total += dot_t(spread_h[:, o * C2 : (o + 1) * C2], down_weight[o])
    hidden_grad[...] = total
    def pick_local(step, carry):
        for i in range(2):
            k = step * 2 + i
            z_all[k] = dot(pick_matrix(wide_x[k], 0, 4), table[0:HALF, :]).astype(BF)
        return carry

    lax.fori_loop(0, EARLY, pick_local, 0)
    pre[...] = dot(features[...], conv_weight[G])
    child_pick[...] = list_matrix(child_rows[...], CAP2)
    turned_features[...] = features[...].T
    send_x.wait_recv()
    for s in range(S):
        table[pl.ds(HALF + (s % 2) * CAP, CAP), pl.ds((s // 2) * C, C)] = in_x[s]

    def multiply(k, group):
        weights = conv_weight[pl.ds(k, len(group))].reshape(len(group) * C, C)
        pre[...] += dot(jnp.concatenate(group, axis=1), weights)

    def forward_early(step, carry):
        group = []
        for i in range(2):
            k = step * 2 + i
            codes = wide_x[k]
            both = dot(pick_matrix(codes, 4, 5), table[HALF:PAIRS, :]).astype(BF) + z_all[k]
            rows = jnp.where(codes < 0, both[:, C:], both[:, :C])
            picked[k] = rows
            group.append(rows)
        multiply(step * 2, group)
        return carry

    lax.fori_loop(0, EARLY, forward_early, 0)

    def forward(step, carry):
        first = EARLY * 2 + step * 6
        group = []
        for i in range(6):
            codes = wide_x[first + i]
            rows = pick_side(dot(pick_matrix(codes), table[...]), codes)
            picked[first + i] = rows
            group.append(rows)
        multiply(first, group)
        return carry

    lax.fori_loop(0, (G - EARLY * 2) // 6, forward, 0)

    act = pre[...]
    gate = jax.nn.sigmoid(act)
    hidden[...] = (features[...].astype(F32) + act * gate).astype(BF)
    chosen = t_dot(child_pick[...], hidden[...]).astype(BF)
    for s in range(S):
        out_h[s] = chosen[s * CAP2 : (s + 1) * CAP2]
    send_h = copies(2, out_h, in_h, 1)
    send_spread.wait_recv()
    turned_hidden = hidden[...].T
    turned_chosen = chosen.T
    for o in range(O):
        at = slice(o * C2, (o + 1) * C2)
        back_spread = jnp.concatenate([in_spread[s, :, at] for s in range(S)], axis=0)
        products = (dot(turned_hidden, spread_h[:, at]) + dot(turned_chosen, back_spread)).astype(BF)
        put_block(28 + 2 * o, products[:, 0:C])
        put_block(29 + 2 * o, products[:, C : 2 * C])
    sum_turn(0, (2,))

    returned = jnp.zeros((S * CAP2, C), F32)
    for o in range(O):
        back_spread = jnp.concatenate([in_spread[s, :, o * C2 : (o + 1) * C2] for s in range(S)], axis=0)
        returned += dot_t(back_spread, down_weight[o])
    grad_h = hidden_grad[...] + dot(child_pick[...], returned.astype(BF))
    hidden_grad[...] = grad_h
    pre_grad[...] = (grad_h * (gate * (1.0 + act * (1.0 - gate)))).astype(BF)

    turned_grad = pre_grad[...].T
    put_block(SELF, dot(turned_features[...], pre_grad[...]).astype(BF))
    for k in range(0, G, 2):
        products = dot(turned_grad, jnp.concatenate([picked[k], picked[k + 1]], axis=1))
        for i in range(2):
            put_block(G if k + i == SELF else k + i, products[:, i * C : (i + 1) * C].T.astype(BF))
        if k == 14:
            sum_turn(0, (0,))
            sum_turn(1, (2,))
    put_block(K, jnp.zeros((C, C), BF))
    sum_turn(0, (1,))
    sum_turn(1, (0,))

    back_x[...] = jnp.zeros_like(back_x)

    def backward_group(first, count):
        weights = conv_weight[pl.ds(first, count)].reshape(count * C, C)
        z = dot_t(pre_grad[...], weights).astype(BF)
        total = back_x[HALF:PAIRS, :]
        for i in range(count):
            z2 = two_sides(z[:, i * C : (i + 1) * C], wide_x[first + i])
            z_all[first + i] = z2
            total += dot(spread_matrix(codes_x[pl.ds(first + i, 1), :], HALF, 128), z2)
        back_x[HALF:PAIRS, :] = total

    def backward(step, carry):
        backward_group(step * 4, 4)
        return carry

    backward_group(G - 2, 2)
    sum_turn(1, (1,))
    lax.fori_loop(0, G // 4, backward, 0)
    for s in range(S):
        out_gx[s] = back_x[pl.ds(HALF + (s % 2) * CAP, CAP), pl.ds((s // 2) * C, C)].astype(BF)
    send_gx = copies(3, out_gx, in_gx, -1)

    def backward_local_group(first, count):
        total = back_x[0:HALF, :]
        for i in range(count):
            total += dot(spread_matrix(codes_x[pl.ds(first + i, 1), :], 0, HALF), z_all[first + i])
        back_x[0:HALF, :] = total

    def backward_local(step, carry):
        backward_local_group(step * 4, 4)
        return carry

    sum_turn(2, (2, 0, 1))
    lax.fori_loop(0, LOCAL_FIRST, backward_local, 0)
    sum_turn(3, (2, 0, 1))

    turned_codes = row_codes(child_map[...], V + S * CAP2, False).T.astype(BF)
    for o in range(0, O, 2):
        wide = dot(turned_codes, unit_rows(O, o, 2)).astype(BF)
        for i in range(2):
            wide_h[pl.ds((o + i) * PD, PD), :] = wide[:, i * 128 : (i + 1) * 128]
    table[0:HALF, 0:C] = hidden[0:HALF, :]
    table[0:HALF, C : 2 * C] = hidden[HALF:V, :]
    table[HALF:PAIRS, C : 2 * C] = jnp.zeros((128, C), BF)
    send_h.wait_recv()
    for s in range(S):
        table[pl.ds(HALF + s * CAP2, CAP2), 0:C] = in_h[s]
    total = jnp.zeros((PD, C2), F32)
    for o in range(O):
        codes = wide_h[pl.ds(o * PD, PD), :]
        rows = pick_side(dot(pick_matrix(codes), table[...]), codes)
        total += dot(rows, down_weight[o])
    coarse[...] = total.astype(BF)


    lax.fori_loop(LOCAL_FIRST, G // 4, backward_local, 0)
    backward_local_group(G - 2, 2)
    hidden_grad[...] += dot_t(pre_grad[...], conv_weight[G])

    sum_turn(4, (2, 0, 1))
    send_gx.wait_recv()
    returned = dot(list_matrix(halo_rows[...], CAP), jnp.concatenate([in_gx[s] for s in range(S)], axis=0))
    local_back = jnp.concatenate([back_x[0:HALF, 0:C], back_x[0:HALF, C : 2 * C]], axis=0)
    input_grad[...] = hidden_grad[...] + local_back + returned

    sum_turn(5, (2, 0, 1))
    for group in flying:
        group.wait_send()


FINISH = [(0, a, a + 4) for a in (0, 4, 8, 12)] + [(1, 0, 4), (1, 4, 8), (1, 8, 11)] + [(2, a, a + 4) for a in (0, 4, 8, 12)]


def finish(
    grad_scale, coarse_in, input_grad_in, summed, coarse, input_grad, conv_grad, down_grad, conv_held, down_held, out_sems
):
    stores = []

    def store(held, out):
        stores.append(pltpu.make_async_copy(held, out, out_sems.at[len(stores)]))
        stores[-1].start()

    store(input_grad_in, input_grad)
    store(coarse_in, coarse)
    for part, first, end in FINISH:
        for block in range(first, end):
            value = summed[part, block * C : (block + 1) * C, :].astype(F32) * grad_scale
            if part < 2:
                conv_held[part * 16 + block] = value
            else:
                down_held[block // 2, :, block % 2 * C : (block % 2 + 1) * C] = value
        if part < 2:
            rows = pl.ds(part * 16 + first, end - first)
            store(conv_held.at[rows], conv_grad.at[rows])
        else:
            rows = pl.ds(first // 2, (end - first) // 2)
            store(down_held.at[rows], down_grad.at[rows])
    for copy in stores:
        copy.wait()


def local(features, conv_weight, down_weight, neighbour_map, halo_rows, child_map, child_rows, out_grad):
    devices = lax.axis_size("shard")
    inputs = (features, conv_weight, down_weight, neighbour_map, halo_rows, child_map, child_rows, out_grad)
    coarse, input_grad, summed = pl.pallas_call(
        kernel,
        out_shape=(
            pltpu.VMEM((PD, C2), BF),
            pltpu.VMEM((V, C), F32),
            pltpu.VMEM((3, 2048, C), BF),
        ),
        in_specs=[pl.BlockSpec(memory_space=pl.ANY)] * 8,
        out_specs=[pl.BlockSpec(memory_space=pltpu.VMEM)] * 3,
        scratch_shapes=[pltpu.VMEM(value.shape, value.dtype) for value in inputs] + [
            pltpu.SemaphoreType.DMA((11,)),
            pltpu.VMEM((32, V), F32),
            pltpu.VMEM((G, V, 128), BF),
            pltpu.VMEM((O * PD, 128), BF),
            pltpu.VMEM((G, V, C), BF),
            pltpu.VMEM((PAIRS, 2 * C), BF),
            pltpu.VMEM((V, C), F32),
            pltpu.VMEM((V, C), BF),
            pltpu.VMEM((V, C), F32),
            pltpu.VMEM((V, C), BF),
            pltpu.VMEM((G, V, 2 * C), BF),
            pltpu.VMEM((PAIRS, 2 * C), F32),
            pltpu.VMEM((V, O * C2), BF),
            pltpu.VMEM((S, CAP, C), BF),
            pltpu.VMEM((S, CAP, C), BF),
            pltpu.VMEM((S, CAP2, C), BF),
            pltpu.VMEM((S, CAP2, C), BF),
            pltpu.VMEM((S, CAP2, O * C2), BF),
            pltpu.VMEM((S, CAP2, O * C2), BF),
            pltpu.VMEM((S, CAP, C), BF),
            pltpu.VMEM((S, CAP, C), BF),
            pltpu.SemaphoreType.DMA((4,)),
            pltpu.SemaphoreType.DMA((4,)),
            pltpu.VMEM((3, 2, 1024, C), BF),
            pltpu.VMEM((3, 1024, C), BF),
            pltpu.VMEM((3, 16, 64, C), BF),
            pltpu.VMEM((3, 15, 64, C), BF),
            pltpu.VMEM((3, 4, 64, C), F32),
            pltpu.SemaphoreType.DMA((5, 3)),
            pltpu.SemaphoreType.DMA((5, 3)),
            pltpu.VMEM((V, S * CAP2), BF),
            pltpu.VMEM((C, V), BF),
        ],
        compiler_params=pltpu.CompilerParams(
            collective_id=0, has_side_effects=True, vmem_limit_bytes=52 * 2**20
        ),
    )(*inputs)
    grad_scale = 1.0 / math.sqrt(V * devices)
    return pl.pallas_call(
        lambda *refs: finish(grad_scale, *refs),
        out_shape=(
            jax.ShapeDtypeStruct((PD, C2), BF),
            jax.ShapeDtypeStruct((V, C), F32),
            jax.ShapeDtypeStruct((K, C, C), F32),
            jax.ShapeDtypeStruct((O, C, C2), F32),
        ),
        in_specs=[pl.BlockSpec(memory_space=pltpu.VMEM)] * 3,
        out_specs=[pl.BlockSpec(memory_space=pl.ANY)] * 4,
        scratch_shapes=[
            pltpu.VMEM((K, C, C), F32),
            pltpu.VMEM((O, C, C2), F32),
            pltpu.SemaphoreType.DMA((len(FINISH) + 2,)),
        ],
        compiler_params=pltpu.CompilerParams(vmem_limit_bytes=52 * 2**20),
    )(*[pltpu.with_memory_space_constraint(value, pltpu.VMEM) for value in (coarse, input_grad, summed)])


def solution(mesh):
    return jax.shard_map(
        local,
        mesh=mesh,
        in_specs=(
            P("shard", None),
            P(),
            P(),
            P(None, "shard"),
            P(None, "shard"),
            P(None, "shard"),
            P(None, "shard"),
            P("shard", None),
        ),
        out_specs=(P("shard", None), P("shard", None), P(), P()),
        check_vma=False,
    )
```
